32 devices in a mesh: seq: 8 (over z, y), tensor: 4 (over x, core).
Axes of the slice: x: 2, y: 2, z: 4, core: 2. Of those that a mesh axis runs over, the one named last changes fastest.
Arguments:
- hidden: bfloat16 [2048, 2048], P(('seq', 'tensor')), may hold values from -6 to 6
- attn_gain: float32 [2048], replicated, may hold values from 0.25 to 1.75
- attn_query: bfloat16 [2048, 2048], P(None, 'tensor'), may hold values from -0.015625 to 0.015625
- attn_key: bfloat16 [2048, 2048], P(None, 'tensor'), may hold values from -0.125 to 0.125
- attn_value: bfloat16 [2048, 2048], P(None, 'tensor'), may hold values from -0.125 to 0.125
- attn_out: bfloat16 [2048, 2048], P('tensor'), may hold values from -0.125 to 0.125
- ff_gain: float32 [2048], replicated, may hold values from 0.25 to 1.75
- ff_gate: bfloat16 [2048, 5120], P(None, 'tensor'), may hold values from -0.125 to 0.125
- ff_up: bfloat16 [2048, 5120], P(None, 'tensor'), may hold values from -0.125 to 0.125
- ff_down: bfloat16 [5120, 2048], P('tensor'), may hold values from -0.078125 to 0.078125
- final_gain: float32 [2048], replicated, may hold values from 0.25 to 1.75
- embedding: bfloat16 [32128, 2048], P('seq', 'tensor'), may hold values from -0.375 to 0.375
- rel_weight: float32 [32, 32], P(None, 'tensor'), may hold values from -6 to 6
- bucket_table: int32 [2048], replicated, may hold values from 0 to 31
- prefix_kv: bfloat16 [2, 32, 256, 2048], P(None, 'seq', None, 'tensor'), may hold values from -1600 to 1600, as said below
- node_lengths: int32 [32], replicated, may hold values from 1 to 256, 3072 in all
- group_branch: int32 [24], replicated, may hold values from 0 to 6
- node_slot: int32 [32], replicated, may hold values from 0 to 31, each once
- request_group: int32 [8], replicated, may hold values from 0 to 23
Outputs:
- hidden_out: bfloat16 [2048, 2048], P(('seq', 'tensor'))
- last_rms: float32 [8], replicated
- top_logit: float32 [8], replicated
The draws below stay inside these ranges and needn't reach their ends.
Inputs may be any that keep to these rules, and one draw needn't show every extreme that they name: `prefix_kv`: finite entries.
All inputs are finite; a program needn't handle non-finite values.
Results may differ from the reference program's by a relative error of at most 0.018.
The reference program's roundings to bfloat16 on the way count: a program that leaves them out, or rounds other values in their place, can miss the bound.
Values may be sent and summed in bfloat16 or wider, within the bound.
No kernel may reach another device: no remote copies, remote signals or barrier semaphores. Data moves between devices by JAX's collectives and lax.ppermute only.
A program may use at most 192 MiB of HBM per device.

```python
import math
import jax
import jax.numpy as jnp
import numpy as np
from jax import lax

D = 2048
HEADS = 32
DH = 64
FF = 5120
VOCAB = 32128
NB = 32
SUF = 256
CAP = 256
BRANCHES = 7
GROUPS = 24
NODES = 32
REQUESTS = 8
TOKENS = 2048
RELS = 2048


def draw_prefix_kv(key, part):
    shape_all = (2, NODES, CAP, HEADS * DH)
    return jnp.clip(jax.random.normal(key, shape_all, jnp.float32), -6.0, 6.0).astype(jnp.bfloat16)


def plant(drawn, own_key, least, largest):
    place = [jax.random.randint(jax.random.fold_in(own_key, axis), (), 0, length) for axis, length in enumerate(drawn.shape)]
    longest = drawn.shape.index(max(drawn.shape))
    beside = place[:longest] + [(place[longest] + 1) % drawn.shape[longest]] + place[longest + 1:]
    return drawn.at[tuple(place)].set(least).at[tuple(beside)].set(largest)


def level_of(own_key, shape, shards, smallest, high):
    def one(axis_at, blocks):
        draws = jax.random.uniform(jax.random.fold_in(jax.random.fold_in(own_key, 6), axis_at), (blocks,), jnp.float32, smallest / len(shards), high / len(shards))
        return jnp.repeat(jnp.exp(draws), shape[axis_at] // blocks).reshape((-1,) + (1,) * (len(shape) - axis_at - 1))

    loudness = one(*shards[0])
    for cut in shards[1:]:
        loudness = loudness * one(*cut)
    return loudness


def split_up(count, total, reach, lean):
    portions = [(1 << 20) // math.isqrt(grade ** lean) + 1 for grade in range(2, count + 1)]
    surplus, given = total - reach - (count - 1), [1] * (count - 1)
    while surplus > 0:
        movable = [i for i in range(count - 1) if given[i] < reach]
        mass, left = sum([portions[i] for i in movable]), surplus
        for i in movable:
            more = min(reach - given[i], max(1, left * portions[i] // mass), surplus)
            given[i] = given[i] + more
            surplus = surplus - more
    return np.array([reach] + given)


def uneven(stream_key, number_of, total, limit, lean):
    if number_of == 2:
        one = jax.random.randint(stream_key, (), max(1, total - limit), min(limit, total - 1) + 1)
        return jnp.stack([one, total - one])
    tallies = jnp.asarray(split_up(number_of, total, limit, lean), jnp.int32)
    pairs = (number_of - 1) // 2
    giver, sink = tallies[1:1 + 2 * pairs:2], tallies[2:2 + 2 * pairs:2]
    margin = jnp.minimum(giver - 1, limit - sink)
    moved = jax.random.randint(jax.random.fold_in(stream_key, 1), (pairs,), 0, 1 << 20) % (margin + 1)
    tallies = tallies.at[1:1 + 2 * pairs:2].set(giver - moved).at[2:2 + 2 * pairs:2].set(sink + moved)
    return tallies[jax.random.permutation(jax.random.fold_in(stream_key, 2), number_of)]


def gaussian(key, shape, spread, limit, pieces=(), kind=jnp.bfloat16):
    values = spread * jax.random.normal(key, shape, jnp.float32)
    if pieces:
        values = values * level_of(key, shape, pieces, -0.22, 0.18)
    return jnp.clip(values, -limit, limit).astype(kind)


def setup_inputs(seed: int = 0) -> dict:
    streams_of = jax.random.split(jax.random.key(seed), 20)
    return {
        "hidden": gaussian(streams_of[0], (TOKENS, D), 1.0, 6.0, ((0, 32),)),
        "attn_gain": jnp.clip(1.0 + 0.15 * jax.random.normal(streams_of[1], (D,), jnp.float32), 0.25, 1.75),
        "attn_query": gaussian(streams_of[2], (D, HEADS * DH), (D * DH) ** -0.5, 0.015625, ((1, 4),)),
        "attn_key": gaussian(streams_of[3], (D, HEADS * DH), D ** -0.5, 0.125, ((1, 4),)),
        "attn_value": gaussian(streams_of[4], (D, HEADS * DH), D ** -0.5, 0.125, ((1, 4),)),
        "attn_out": gaussian(streams_of[5], (HEADS * DH, D), (HEADS * DH) ** -0.5, 0.125, ((0, 4),)),
        "ff_gain": jnp.clip(1.0 + 0.15 * jax.random.normal(streams_of[6], (D,), jnp.float32), 0.25, 1.75),
        "ff_gate": gaussian(streams_of[7], (D, FF), D ** -0.5, 0.125, ((1, 4),)),
        "ff_up": gaussian(streams_of[8], (D, FF), D ** -0.5, 0.125, ((1, 4),)),
        "ff_down": gaussian(streams_of[9], (FF, D), FF ** -0.5, 0.078125, ((0, 4),)),
        "final_gain": jnp.clip(1.0 + 0.15 * jax.random.normal(streams_of[10], (D,), jnp.float32), 0.25, 1.75),
        "embedding": gaussian(streams_of[11], (VOCAB, D), (D // 9) ** -0.5, 0.375, ((0, 8), (1, 4))),
        "rel_weight": gaussian(streams_of[12], (NB, HEADS), 1.0, 6.0, ((1, 4),), jnp.float32),
        "bucket_table": plant(jax.random.randint(streams_of[13], (RELS,), 0, NB), jax.random.fold_in(streams_of[13], 1), 0, NB - 1).astype(jnp.int32),
        "prefix_kv": draw_prefix_kv(jax.random.fold_in(streams_of[19], 71), 0),
        "node_lengths": uneven(streams_of[15], NODES, 12 * CAP, CAP, 2).astype(jnp.int32),
        "group_branch": plant(jax.random.randint(streams_of[16], (GROUPS,), 0, BRANCHES), jax.random.fold_in(streams_of[16], 1), 0, BRANCHES - 1).astype(jnp.int32),
        "node_slot": jax.random.permutation(streams_of[17], NODES).astype(jnp.int32),
        "request_group": plant(jax.random.randint(streams_of[18], (REQUESTS,), 0, GROUPS), jax.random.fold_in(streams_of[18], 1), 0, GROUPS - 1).astype(jnp.int32),
    }


def rms_scale(values, gain):
    widened = values.astype(jnp.float32)
    mean_square = lax.optimization_barrier(jnp.mean(widened * widened, axis=-1, keepdims=True))
    return widened * lax.rsqrt(mean_square + 1e-06) * gain

def attend(queries, key_rows, value_rows, table_bias, query_base, key_start, key_count):
    query_count = queries.shape[0]
    key_span = key_rows.shape[0]
    offset = table_bias.shape[1] // 2
    first_col = (offset + key_start - query_base - (query_count - 1)).astype(jnp.int32)
    bias_slab = lax.dynamic_slice_in_dim(table_bias, first_col, key_span + query_count - 1, 1)
    lookup = jnp.arange(key_span)[None, :] - jnp.arange(query_count)[:, None] + (query_count - 1)
    bias_block = jnp.take(bias_slab, lookup, axis=1)
    scores = jnp.einsum('qhe,khe->hqk', queries.astype(jnp.float32), key_rows.astype(jnp.float32)) + bias_block
    is_valid = jnp.arange(key_span) < key_count
    scores = jnp.where(is_valid[None, None, :], scores, -1e+30)
    row_peak = lax.optimization_barrier(jnp.max(scores, axis=2))
    weights = jnp.exp(scores - row_peak[:, :, None])
    row_total = lax.optimization_barrier(jnp.sum(weights, axis=2))
    rounded = lax.optimization_barrier(weights.astype(jnp.bfloat16))
    weighted = jnp.einsum('hqk,khe->qhe', rounded.astype(jnp.float32), value_rows.astype(jnp.float32))
    output = (weighted / jnp.transpose(row_total)[:, :, None]).astype(jnp.bfloat16)
    return (output, jnp.transpose(row_peak), jnp.transpose(row_total))

def combine_parts(outputs, peaks, totals):
    highest = lax.optimization_barrier(jnp.max(peaks, axis=0, keepdims=True))
    scales = totals * jnp.exp(peaks - highest)
    numer = lax.optimization_barrier(jnp.sum(scales[..., None] * outputs.astype(jnp.float32), axis=0))
    return numer / lax.optimization_barrier(jnp.sum(scales, axis=0))[..., None]

def reference(hidden, attn_gain, attn_query, attn_key, attn_value, attn_out, ff_gain, ff_gate, ff_up, ff_down, final_gain, embedding, rel_weight, bucket_table, prefix_kv, node_lengths, group_branch, node_slot, request_group):
    normed = rms_scale(hidden, attn_gain).astype(jnp.bfloat16)
    query_all = jnp.dot(normed, attn_query, preferred_element_type=jnp.float32).astype(jnp.bfloat16)
    key_all = jnp.dot(normed, attn_key, preferred_element_type=jnp.float32).astype(jnp.bfloat16)
    value_all = jnp.dot(normed, attn_value, preferred_element_type=jnp.float32).astype(jnp.bfloat16)
    table_bias = jnp.transpose(rel_weight[bucket_table])
    shaped = (REQUESTS, SUF, HEADS, DH)
    query_req = query_all.reshape(shaped)
    key_req = key_all.reshape(shaped)
    value_req = value_all.reshape(shaped)

    def per_request(request):
        group_id = request_group[request]
        branch = 1 + group_branch[group_id]
        group_node = 1 + BRANCHES + group_id
        path_nodes = jnp.stack([jnp.zeros_like(group_id), branch, group_node])
        path_counts = node_lengths[path_nodes]
        path_starts = jnp.stack([jnp.zeros_like(path_counts[0]), path_counts[0], path_counts[0] + path_counts[1]])
        base_pos = jnp.sum(path_counts)
        own_query = query_req[request]
        part_outs = []
        part_peaks = []
        part_totals = []
        for level_idx in range(3):
            slot_kv = prefix_kv[:, node_slot[path_nodes[level_idx]]]
            cache_keys = slot_kv[0].reshape(CAP, HEADS, DH)
            cache_values = slot_kv[1].reshape(CAP, HEADS, DH)
            output, row_peak, row_total = attend(own_query, cache_keys, cache_values, table_bias, base_pos, path_starts[level_idx], path_counts[level_idx])
            part_outs.append(output)
            part_peaks.append(row_peak)
            part_totals.append(row_total)
        output, row_peak, row_total = attend(own_query, key_req[request], value_req[request], table_bias, base_pos, base_pos, SUF)
        part_outs.append(output)
        part_peaks.append(row_peak)
        part_totals.append(row_total)
        merged = combine_parts(jnp.stack(part_outs), jnp.stack(part_peaks), jnp.stack(part_totals))
        return merged.astype(jnp.bfloat16).reshape(SUF, HEADS * DH)
    attn = lax.map(per_request, jnp.arange(REQUESTS)).reshape(TOKENS, HEADS * DH)
    mid = (hidden.astype(jnp.float32) + jnp.dot(attn, attn_out, preferred_element_type=jnp.float32)).astype(jnp.bfloat16)
    normed_mid = rms_scale(mid, ff_gain).astype(jnp.bfloat16)
    gate_part = jnp.dot(normed_mid, ff_gate, preferred_element_type=jnp.float32)
    up_part = jnp.dot(normed_mid, ff_up, preferred_element_type=jnp.float32)
    inner = (jax.nn.gelu(gate_part, approximate=True) * up_part).astype(jnp.bfloat16)
    hidden_out = (mid.astype(jnp.float32) + jnp.dot(inner, ff_down, preferred_element_type=jnp.float32)).astype(jnp.bfloat16)
    last_rows = hidden_out[SUF - 1::SUF].astype(jnp.float32)
    mean_square = lax.optimization_barrier(jnp.mean(last_rows * last_rows, axis=1))
    last_rms = jnp.sqrt(mean_square)
    final_rows = (last_rows * lax.rsqrt(mean_square + 1e-06)[:, None] * final_gain).astype(jnp.bfloat16)
    logits = jnp.dot(final_rows, jnp.transpose(embedding), preferred_element_type=jnp.float32)
    top_logit = lax.optimization_barrier(jnp.max(logits, axis=1))
    return (hidden_out, last_rms, top_logit)
```

```python
import functools

import jax
import jax.numpy as jnp
from jax import lax
from jax.experimental import pallas as pl
from jax.experimental.pallas import tpu as pltpu
from jax.sharding import PartitionSpec as P

BRANCHES = 7
HEAD = 64
GRAIN = 16
STAGES = 4
MIB = 1 << 20
CLASSES = (
    (256, 224, 160, 64),
    (288, 272, 256, 128),
    (352, 320, 272, 256),
    (448, 384, 320, 272),
    (576, 512, 400, 352),
)


def rms_scale(values, gain):
    widened = values.astype(jnp.float32)
    mean_square = jnp.mean(widened * widened, axis=-1, keepdims=True)
    return widened * lax.rsqrt(mean_square + 1e-06) * gain


def xor_pairs(size, mask):
    return [(i, i ^ mask) for i in range(size)]


def ring_place(index, size):
    half = lax.shift_right_logical(index, jnp.int32(1))
    return jnp.where(lax.bitwise_and(index, jnp.int32(1)) == 0, half, size - 1 - half)


def ring_pairs(size, step):
    order = list(range(0, size, 2)) + list(range(1, size, 2))[::-1]
    return [(order[i], order[(i + step) % size]) for i in range(size)]


def block_order(size):
    bits = size.bit_length() - 1
    return sorted(range(size), key=lambda i: -int(format(i, "b").zfill(bits)[::-1], 2))


def iota(shape, axis):
    return lax.broadcasted_iota(jnp.int32, shape, axis)


def plan_kernel(n_seq, slots_here, cap, classes, lengths, slots, branch_of, groups, table):
    nodes = lengths.shape[1]
    requests = groups.shape[1]
    hop_group = -(-(n_seq // 2) // STAGES)
    eye = iota((nodes, nodes), 0) == iota((nodes, nodes), 1)

    def column(row):
        return jnp.sum(jnp.where(eye, row, 0), axis=1, keepdims=True)

    length = lengths[...]
    slot = slots[...]
    owner = jnp.zeros_like(slot)
    for k in range(1, n_seq):
        owner = owner + (slot >= k * slots_here).astype(jnp.int32)
    inner_slot = slot - owner * slots_here
    place = ring_place(owner, n_seq)
    req_eye = iota((requests, requests), 0) == iota((requests, requests), 1)
    group = jnp.sum(jnp.where(req_eye, groups[...], 0), axis=1, keepdims=True)
    n_groups = branch_of.shape[1]
    branch = jnp.sum(
        jnp.where(iota((requests, n_groups), 1) == group, branch_of[...], 0), axis=1, keepdims=True
    )
    node = iota((requests, nodes), 1)
    need = (node == 0) | (node == 1 + branch) | (node == 1 + BRANCHES + group)
    seats = ring_place(iota((requests, nodes), 0), n_seq)
    ahead = seats - place
    ahead = jnp.where(ahead < 0, ahead + n_seq, ahead)
    best = jnp.full((1, nodes), 1 << 20, jnp.int32)
    forth = jnp.zeros((1, nodes), jnp.int32)
    back = jnp.zeros((1, nodes), jnp.int32)
    for cut in range(n_seq):
        a = jnp.max(jnp.where(need & (ahead <= cut), ahead, 0), axis=0, keepdims=True)
        b = jnp.max(jnp.where(need & (ahead > cut), n_seq - ahead, 0), axis=0, keepdims=True)
        key = jnp.maximum(a, b) * 128 + a + b
        better = key < best
        best = jnp.where(better, key, best)
        forth = jnp.where(better, a, forth)
        back = jnp.where(better, b, back)
    grains = lax.shift_right_logical(length + (GRAIN - 1), jnp.int32(4))
    grains_col = column(grains)
    place_col = column(place)
    earlier = iota((nodes, nodes), 0) < iota((nodes, nodes), 1)
    mine = iota((n_seq, nodes), 0) == place
    offsets = []
    stages = []
    needs = [jnp.zeros((1, 1), jnp.int32)] * STAGES
    for hops in (forth, back):
        stage = jnp.zeros_like(hops)
        for j in range(STAGES):
            stage = stage + (hops > j * hop_group).astype(jnp.int32)
        stage_col = column(stage)
        ahead_of = (stage_col > stage) | ((stage_col == stage) & earlier)
        counted = (place_col == place) & (stage_col > 0) & ahead_of
        offsets.append(jnp.sum(jnp.where(counted, grains_col, 0), axis=0, keepdims=True))
        stages.append(stage)
        for j in range(STAGES):
            rows = jnp.sum(jnp.where(mine & (stage > j), grains, 0), axis=1, keepdims=True)
            needs[j] = jnp.maximum(needs[j], jnp.max(rows, axis=0, keepdims=True))
    choice = jnp.full((1, 1), len(classes) - 1, jnp.int32)
    for number in range(len(classes) - 2, -1, -1):
        fits = needs[0] * GRAIN <= classes[number][0]
        for j in range(1, STAGES):
            fits = fits & (needs[j] * GRAIN <= classes[number][j])
        choice = jnp.where(fits, number, choice)
    table[...] = jnp.zeros_like(table)
    rows = [length, place, forth, back, offsets[0], offsets[1], inner_slot]
    for number, row in enumerate(rows):
        table[number : number + 1, :nodes] = row
    table[7:8, :] = jnp.broadcast_to(choice, (1, table.shape[1]))


def spans(caps):
    edges = [0] + [caps[j] // GRAIN for j in range(STAGES - 1, -1, -1)]
    return [
        (edges[i], edges[i + 1], STAGES - i) for i in range(STAGES) if edges[i + 1] > edges[i]
    ]


def pack_kernel(n_seq, nodes, parts, table, cache, *outs):
    here = ring_place(lax.axis_index("seq"), n_seq)
    width = cache.shape[3]

    def one_node(n, carry):
        @pl.when(table[1, n] == here)
        def _():
            slot = table[6, n]
            count = lax.shift_right_logical(table[0, n] + (GRAIN - 1), 4)
            for way in range(2):
                reach = table[2 + way, n]
                first = table[4 + way, n]
                for number, (low, high, _) in enumerate(parts):
                    target = outs[way * len(parts) + number]
                    start = jnp.maximum(low - first, 0)
                    stop = jnp.where(reach > 0, jnp.minimum(high - first, count), 0)

                    def one_grain(i, inner, target=target, first=first, low=low):
                        source = pl.ds(pl.multiple_of(i * GRAIN, GRAIN), GRAIN)
                        place = pl.ds(pl.multiple_of((first + i - low) * GRAIN, GRAIN), GRAIN)
                        target[place, :width] = cache[0, slot, source, :]
                        target[place, width:] = cache[1, slot, source, :]
                        return inner

                    lax.fori_loop(start, stop, one_grain, 0)

        return carry

    lax.fori_loop(0, nodes, one_node, 0)


def attention_kernel(
    n_seq, n_tensor, order, parts, hop_group, table, groups, branch_of, buckets, weights, proj, cache, *rest
):
    n_landed = len(rest) - 4
    landed, out, own, kept, bias = rest[:n_landed], *rest[n_landed:]
    seq_index = lax.axis_index("seq")
    tensor_index = lax.axis_index("tensor")
    here = ring_place(seq_index, n_seq)
    rows, width = out.shape
    heads = width // HEAD
    cap = cache.shape[2]
    block = rows // n_tensor
    for number, which in enumerate(order):
        seat = lax.bitwise_xor(tensor_index, jnp.int32(which))
        own[pl.ds(pl.multiple_of(seat * block, block), block), :] = proj[
            number * block : (number + 1) * block, :
        ]
    kept[...] = jnp.zeros_like(kept)
    group = groups[0, seq_index]
    path = [jnp.int32(0), 1 + branch_of[0, group], 1 + BRANCHES + group]
    counts = [table[0, n] for n in path]
    starts = [jnp.int32(0), counts[0], counts[0] + counts[1]]
    base = counts[0] + counts[1] + counts[2]
    for level, n in enumerate(path):
        count = lax.shift_right_logical(counts[level] + (GRAIN - 1), 4)
        ahead = here - table[1, n]
        ahead = jnp.where(ahead < 0, ahead + n_seq, ahead)
        local = ahead == 0
        slot = table[6, n]
        forward = ahead <= table[2, n]

        def from_cache(i, inner, level=level, slot=slot):
            place = pl.ds(pl.multiple_of(i * GRAIN, GRAIN), GRAIN)
            kept[level, place, :width] = cache[0, slot, place, :]
            kept[level, place, width:] = cache[1, slot, place, :]
            return inner

        lax.fori_loop(0, jnp.where(local, count, 0), from_cache, 0)
        number = 0
        for way in range(2):
            hop = ahead if way == 0 else n_seq - ahead
            this_way = (~local) & (forward if way == 0 else ~forward)
            first = table[4 + way, n]
            for low, high, stage in parts:
                for step in range(1, stage * hop_group + 1):
                    source = landed[number]
                    number += 1
                    here_it_is = this_way & (hop == step)
                    start = jnp.maximum(low - first, 0)
                    stop = jnp.where(here_it_is, jnp.minimum(high - first, count), 0)

                    def from_ring(i, inner, source=source, low=low, first=first, level=level):
                        place = pl.ds(pl.multiple_of(i * GRAIN, GRAIN), GRAIN)
                        taken = pl.ds(pl.multiple_of((first + i - low) * GRAIN, GRAIN), GRAIN)
                        kept[level, place, :] = source[taken, :]
                        return inner

                    lax.fori_loop(start, stop, from_ring, 0)
    rels = buckets.shape[1]
    bucket = jnp.broadcast_to(buckets[...], (heads, rels))
    reversed_bias = jnp.zeros((heads, rels), jnp.float32)
    for b in range(weights.shape[1]):
        reversed_bias = jnp.where(bucket == b, weights[:, b : b + 1], reversed_bias)
    half = rels // 2
    window = 2 * rows
    for part in range(4):
        shift = (starts[part] - base) if part < 3 else jnp.int32(0)
        turn = half + 1 + shift
        turned = pltpu.roll(reversed_bias, lax.rem(turn + rels, rels), 1)
        bias[part] = jnp.concatenate([turned[:, :rows], turned[:, rels - rows :]], axis=1)
    key_row = iota((cap, 2 * rows), 0)
    half_row = iota((2 * HEAD, rows), 0) < HEAD
    for pair in range(heads // 2):
        cols = slice(pair * 2 * HEAD, (pair + 1) * 2 * HEAD)
        query = jnp.transpose(own[:, cols].astype(jnp.float32))
        query = jnp.concatenate(
            [jnp.where(half_row, query, 0.0), jnp.where(half_row, 0.0, query)], axis=1
        ).astype(jnp.bfloat16)
        scores = []
        for part in range(4):
            if part < 3:
                keys = kept[part, :, cols]
            else:
                keys = own[:, width + pair * 2 * HEAD : width + (pair + 1) * 2 * HEAD]
            score = jnp.dot(keys, query, preferred_element_type=jnp.float32)
            slabs = []
            for head in (2 * pair, 2 * pair + 1):
                line = jnp.broadcast_to(bias[part, head : head + 1, :], (rows // 2, window))
                rolled = pltpu.roll(line, 0, 1, stride=1, stride_axis=0)
                slabs.append(
                    jnp.concatenate(
                        [
                            rolled[:, :rows],
                            jnp.concatenate(
                                [rolled[:, window - rows // 2 :], rolled[:, : rows // 2]], axis=1
                            ),
                        ],
                        axis=0,
                    )
                )
            score = score + jnp.concatenate(slabs, axis=1)
            if part < 3:
                score = jnp.where(key_row < counts[part], score, -1e30)
            scores.append(score)
        peak = jnp.max(scores[0], axis=0, keepdims=True)
        for score in scores[1:]:
            peak = jnp.maximum(peak, jnp.max(score, axis=0, keepdims=True))
        total = jnp.zeros_like(peak)
        summed = jnp.zeros((2 * HEAD, 2 * rows), jnp.float32)
        for part in range(4):
            chance = jnp.exp(scores[part] - peak)
            total = total + jnp.sum(chance, axis=0, keepdims=True)
            if part < 3:
                values = kept[part, :, width + pair * 2 * HEAD : width + (pair + 1) * 2 * HEAD]
            else:
                values = own[:, 2 * width + pair * 2 * HEAD : 2 * width + (pair + 1) * 2 * HEAD]
            summed = summed + lax.dot_general(
                values,
                chance.astype(jnp.bfloat16),
                (((0,), (0,)), ((), ())),
                preferred_element_type=jnp.float32,
            )
        scaled = summed / total
        both = jnp.concatenate([scaled[:HEAD, :rows], scaled[HEAD:, rows:]], axis=0)
        result = jnp.transpose(both).astype(jnp.bfloat16)
        own[:, cols] = result
    for number, which in enumerate(order):
        seat = lax.bitwise_xor(tensor_index, jnp.int32(which))
        out[number * block : (number + 1) * block, :] = own[
            pl.ds(pl.multiple_of(seat * block, block), block), :width
        ]


def vmem(count=1):
    return [pl.BlockSpec(memory_space=pltpu.VMEM)] * count


def smem(count=1):
    return [pl.BlockSpec(memory_space=pltpu.SMEM)] * count


def gather_blocks(own, size, order):
    blocks = {0: own}
    for i in sorted(range(1, size), key=lambda i: (bin(i).count("1"), -i)):
        low = i & -i
        blocks[i] = lax.ppermute(blocks[i ^ low], "tensor", xor_pairs(size, low))
    return jnp.concatenate([blocks[i] for i in order], axis=0)


def scatter_sum(rows, weight, size):
    half = rows.shape[0] // 2
    sent = jnp.dot(rows[:half], weight, preferred_element_type=jnp.float32).astype(jnp.bfloat16)
    arrived = lax.ppermute(sent, "tensor", xor_pairs(size, 1))
    total = jnp.dot(rows[half:], weight, preferred_element_type=jnp.float32)
    total = total + arrived.astype(jnp.float32)
    mask = 2
    while mask < size:
        half //= 2
        arrived = lax.ppermute(total[:half].astype(jnp.bfloat16), "tensor", xor_pairs(size, mask))
        total = total[half:] + arrived.astype(jnp.float32)
        mask *= 2
    return total


def attend_branch(
    caps, n_seq, n_tensor, table, normed, attn_query, attn_key, attn_value, buckets, weights, prefix_kv, groups, branch_of
):
    parts = spans(caps)
    hop_group = -(-(n_seq // 2) // STAGES)
    nodes = n_seq * prefix_kv.shape[1]
    width = prefix_kv.shape[3]
    order = block_order(n_tensor)
    sizes = [(high - low) * GRAIN for low, high, _ in parts]
    shapes = [jax.ShapeDtypeStruct((size, 2 * width), jnp.bfloat16) for size in sizes]
    packed = pl.pallas_call(
        functools.partial(pack_kernel, n_seq, nodes, parts),
        out_shape=shapes * 2,
        in_specs=smem() + vmem(),
        out_specs=vmem(2 * len(shapes)),
        compiler_params=pltpu.CompilerParams(vmem_limit_bytes=24 * MIB),
    )(table, prefix_kv)
    landed = []
    for way in range(2):
        pairs = ring_pairs(n_seq, 1 if way == 0 else -1)
        for number, (_, _, stage) in enumerate(parts):
            moving = packed[way * len(parts) + number]
            for _ in range(stage * hop_group):
                moving = lax.ppermute(moving, "seq", pairs)
                landed.append(moving)
    rows = gather_blocks(normed, n_tensor, order)
    proj = jnp.concatenate(
        [
            jnp.dot(rows, weight, preferred_element_type=jnp.float32).astype(jnp.bfloat16)
            for weight in (attn_query, attn_key, attn_value)
        ],
        axis=1,
    )
    n_rows = rows.shape[0]
    cap = prefix_kv.shape[2]
    return pl.pallas_call(
        functools.partial(attention_kernel, n_seq, n_tensor, order, parts, hop_group),
        out_shape=jax.ShapeDtypeStruct((n_rows, width), jnp.bfloat16),
        in_specs=smem(3) + vmem(4 + len(landed)),
        out_specs=vmem()[0],
        scratch_shapes=[
            pltpu.VMEM((n_rows, 3 * width), jnp.bfloat16),
            pltpu.VMEM((3, cap, 2 * width), jnp.bfloat16),
            pltpu.VMEM((4, width // HEAD, 2 * n_rows), jnp.float32),
        ],
        compiler_params=pltpu.CompilerParams(vmem_limit_bytes=48 * MIB),
    )(table, groups, branch_of, buckets, weights, proj, prefix_kv, *landed)


def per_device(
    hidden,
    attn_gain,
    attn_query,
    attn_key,
    attn_value,
    attn_out,
    ff_gain,
    ff_gate,
    ff_up,
    ff_down,
    final_gain,
    embedding,
    rel_weight,
    bucket_table,
    prefix_kv,
    node_lengths,
    group_branch,
    node_slot,
    request_group,
):
    n_seq = lax.axis_size("seq")
    n_tensor = lax.axis_size("tensor")
    tensor_index = lax.axis_index("tensor")
    own_rows, width = hidden.shape
    assert request_group.shape[0] == n_seq
    order = block_order(n_tensor)
    slots_here, cap = prefix_kv.shape[1:3]
    most = slots_here * cap
    classes = []
    for caps in CLASSES + ((most,) * STAGES,):
        caps = tuple(min(c, most) for c in caps)
        if caps not in classes:
            classes.append(caps)
    groups = request_group[None, :]
    branch_of = group_branch[None, :]
    table = pl.pallas_call(
        functools.partial(plan_kernel, n_seq, slots_here, cap, classes),
        out_shape=jax.ShapeDtypeStruct((8, 128), jnp.int32),
        in_specs=vmem(4),
        out_specs=vmem()[0],
    )(node_lengths[None, :], node_slot[None, :], branch_of, groups)
    normed = rms_scale(hidden, attn_gain).astype(jnp.bfloat16)
    attn = lax.switch(
        table[7, 0],
        [functools.partial(attend_branch, caps, n_seq, n_tensor) for caps in classes],
        table,
        normed,
        attn_query,
        attn_key,
        attn_value,
        bucket_table[::-1][None, :],
        jnp.transpose(rel_weight),
        prefix_kv,
        groups,
        branch_of,
    )
    attn_sum = scatter_sum(attn, attn_out, n_tensor)
    mid = (hidden.astype(jnp.float32) + attn_sum).astype(jnp.bfloat16)
    rows = gather_blocks(rms_scale(mid, ff_gain).astype(jnp.bfloat16), n_tensor, order)
    gate_part = jnp.dot(rows, ff_gate, preferred_element_type=jnp.float32)
    up_part = jnp.dot(rows, ff_up, preferred_element_type=jnp.float32)
    inner = (jax.nn.gelu(gate_part, approximate=True) * up_part).astype(jnp.bfloat16)
    ff_summed = scatter_sum(inner, ff_down, n_tensor)
    hidden_out = (mid.astype(jnp.float32) + ff_summed).astype(jnp.bfloat16)
    last = hidden_out[own_rows - 1 :]
    copies = [
        lax.ppermute(last, "tensor", [(n_tensor - 1, i)]) for i in range(n_tensor - 1)
    ]
    last = jnp.where(tensor_index == n_tensor - 1, last, sum(copies[1:], copies[0]))
    seq_index = lax.axis_index("seq")
    shifted = [last] + [
        lax.ppermute(last, "seq", [(i, (i + k) % n_seq) for i in range(n_seq)])
        for k in range(1, n_seq)
    ]
    stacked = jnp.concatenate(shifted, axis=0)
    from_row = lax.rem(seq_index - jnp.arange(n_seq) + n_seq, n_seq)
    last_rows = stacked[from_row].astype(jnp.float32)
    mean_square = jnp.mean(last_rows * last_rows, axis=1)
    last_rms = jnp.sqrt(mean_square)
    final_rows = (last_rows * lax.rsqrt(mean_square + 1e-06)[:, None] * final_gain).astype(
        jnp.bfloat16
    )
    embed_cols = embedding.shape[1]
    columns = lax.dynamic_slice_in_dim(final_rows, tensor_index * embed_cols, embed_cols, 1)
    logits = lax.dot_general(
        columns, embedding, (((1,), (1,)), ((), ())), preferred_element_type=jnp.float32
    )
    mask = 1
    while mask < n_tensor:
        sent = logits.astype(jnp.bfloat16)
        arrived = lax.ppermute(sent, "tensor", xor_pairs(n_tensor, mask))
        logits = sent.astype(jnp.float32) + arrived.astype(jnp.float32)
        mask *= 2
    top = jnp.max(logits, axis=1)
    tops = [top] + [
        lax.ppermute(top, "seq", [(i, (i + k) % n_seq) for i in range(n_seq)])
        for k in range(1, n_seq)
    ]
    top_logit = functools.reduce(jnp.maximum, tops)
    return (hidden_out, last_rms, top_logit)


def solution(mesh):
    return jax.shard_map(
        per_device,
        mesh=mesh,
        in_specs=(
            P(("seq", "tensor"), None),
            P(),
            P(None, "tensor"),
            P(None, "tensor"),
            P(None, "tensor"),
            P("tensor", None),
            P(),
            P(None, "tensor"),
            P(None, "tensor"),
            P("tensor", None),
            P(),
            P("seq", "tensor"),
            P(None, "tensor"),
            P(),
            P(None, "seq", None, "tensor"),
            P(),
            P(),
            P(),
            P(),
        ),
        out_specs=(P(("seq", "tensor"), None), P(), P()),
        check_vma=False,
    )
```

```python
import functools

import jax
import jax.numpy as jnp
from jax import lax
from jax.experimental import pallas as pl
from jax.experimental.pallas import tpu as pltpu
from jax.sharding import PartitionSpec as P

BRANCHES = 7
HEAD = 64
GRAIN = 16
MIB = 1 << 20
PASSED = 160
CLASSES = (448, 320, 256, 224, 192, 160)


def rms_scale(values, gain):
    widened = values.astype(jnp.float32)
    mean_square = jnp.mean(widened * widened, axis=-1, keepdims=True)
    return widened * lax.rsqrt(mean_square + 1e-06) * gain


def xor_pairs(size, mask):
    return [(i, i ^ mask) for i in range(size)]


def ring_place(index, size):
    half = lax.shift_right_logical(index, jnp.int32(1))
    return jnp.where(lax.bitwise_and(index, jnp.int32(1)) == 0, half, size - 1 - half)


def ring_pairs(size, step):
    order = list(range(0, size, 2)) + list(range(1, size, 2))[::-1]
    return [(order[i], order[(i + step) % size]) for i in range(size)]


def block_order(size):
    bits = size.bit_length() - 1
    return sorted(range(size), key=lambda i: -int(format(i, "b").zfill(bits)[::-1], 2))


def iota(shape, axis):
    return lax.broadcasted_iota(jnp.int32, shape, axis)


def plan_kernel(n_seq, slots_here, passed, classes, lengths, slots, branch_of, groups, table):
    nodes = lengths.shape[1]
    requests = groups.shape[1]
    eye = iota((nodes, nodes), 0) == iota((nodes, nodes), 1)
    seq_eye = iota((n_seq, n_seq), 0) == iota((n_seq, n_seq), 1)

    def column(row):
        return jnp.sum(jnp.where(eye, row, 0), axis=1, keepdims=True)

    def seq_row(col):
        return jnp.sum(jnp.where(seq_eye, col, 0), axis=0, keepdims=True)

    slot = slots[...]
    owner = jnp.zeros_like(slot)
    for k in range(1, n_seq):
        owner = owner + (slot >= k * slots_here).astype(jnp.int32)
    place = ring_place(owner, n_seq)
    req_eye = iota((requests, requests), 0) == iota((requests, requests), 1)
    group = jnp.sum(jnp.where(req_eye, groups[...], 0), axis=1, keepdims=True)
    n_groups = branch_of.shape[1]
    branch = jnp.sum(
        jnp.where(iota((requests, n_groups), 1) == group, branch_of[...], 0), axis=1, keepdims=True
    )
    node = iota((requests, nodes), 1)
    need = (node == 0) | (node == 1 + branch) | (node == 1 + BRANCHES + group)
    needed = jnp.max(need.astype(jnp.int32), axis=0, keepdims=True)
    grains = needed * lax.shift_right_logical(lengths[...] + (GRAIN - 1), jnp.int32(4))
    earlier = iota((nodes, nodes), 0) < iota((nodes, nodes), 1)
    before = (column(place) == place) & earlier
    first = jnp.sum(jnp.where(before, column(grains), 0), axis=0, keepdims=True)
    held = jnp.sum(
        jnp.where(iota((n_seq, nodes), 0) == place, grains, 0), axis=1, keepdims=True
    )
    every = jnp.sum(held, axis=0, keepdims=True)
    upto = iota((n_seq, n_seq), 1) <= iota((n_seq, n_seq), 0)
    surplus = n_seq * seq_row(held) - every
    running = jnp.sum(jnp.where(upto, surplus, 0), axis=1, keepdims=True)
    middle = lax.shift_right_arithmetic(
        jnp.max(running, axis=0, keepdims=True) + jnp.min(running, axis=0, keepdims=True),
        jnp.int32(1),
    )
    flow = lax.shift_right_arithmetic(
        running - middle + n_seq // 2, jnp.int32(n_seq.bit_length() - 1)
    )
    most = passed // GRAIN
    flow = jnp.minimum(jnp.maximum(flow, -most), most)
    before_me = iota((n_seq, n_seq), 1) == lax.rem(
        iota((n_seq, n_seq), 0) + (n_seq - 1), jnp.int32(n_seq)
    )
    after_me = iota((n_seq, n_seq), 1) == lax.rem(
        iota((n_seq, n_seq), 0) + 1, jnp.int32(n_seq)
    )

    def from_seat(which, col):
        return jnp.sum(jnp.where(which, seq_row(col), 0), axis=1, keepdims=True)

    onward = jnp.minimum(jnp.maximum(flow, 0), held)
    backward = jnp.minimum(jnp.maximum(-from_seat(before_me, flow), 0), held - onward)
    kept = held - onward - backward
    block = kept + from_seat(before_me, onward) + from_seat(after_me, backward)
    largest = jnp.max(block, axis=0, keepdims=True) * GRAIN
    choice = jnp.zeros((1, 1), jnp.int32)
    for number, rows in enumerate(classes):
        choice = jnp.where(largest <= rows, number, choice)
    table[...] = jnp.zeros_like(table)
    for number, row in enumerate((lengths[...], place, first, slot - owner * slots_here, grains)):
        table[number : number + 1, :nodes] = row
    for number, col in enumerate((onward, backward, kept)):
        table[8 + number : 9 + number, :n_seq] = seq_row(col)
    table[11:12, :] = jnp.broadcast_to(choice, (1, table.shape[1]))


def moved(count, start, stop, copy):
    def step(i, carry):
        copy(i)
        return carry

    lax.fori_loop(jnp.maximum(start, 0), jnp.minimum(stop, count), step, 0)


def grain(i):
    return pl.ds(pl.multiple_of(i * GRAIN, GRAIN), GRAIN)


def pack_kernel(n_seq, nodes, table, cache, onward, backward, kept):
    here = ring_place(lax.axis_index("seq"), n_seq)
    width = cache.shape[3]
    to_next = table[8, here]
    passed = to_next + table[9, here]

    def one_node(n, carry):
        @pl.when((table[1, n] == here) & (table[4, n] > 0))
        def _():
            slot = table[3, n]
            count = table[4, n]
            first = table[2, n]

            def put(target, low):
                def copy(i):
                    target[grain(first + i - low), :width] = cache[0, slot, grain(i), :]
                    target[grain(first + i - low), width:] = cache[1, slot, grain(i), :]

                return copy

            moved(count, 0, to_next - first, put(onward, 0))
            moved(count, to_next - first, passed - first, put(backward, to_next))
            moved(count, passed - first, count, put(kept, passed))

        return carry

    lax.fori_loop(0, nodes, one_node, 0)


def merge_kernel(n_seq, table, kept, from_before, from_after, left, right):
    here = ring_place(lax.axis_index("seq"), n_seq)
    before = lax.rem(here + (n_seq - 1), n_seq)
    after = lax.rem(here + 1, n_seq)
    half = left.shape[0] // GRAIN
    left[...] = kept[: left.shape[0], :]
    right[...] = kept[left.shape[0] :, :]
    at = table[10, here]
    for source, count in ((from_before, table[8, before]), (from_after, table[9, after])):

        def to_left(i, source=source, at=at):
            left[grain(at + i), :] = source[grain(i), :]

        def to_right(i, source=source, at=at):
            right[grain(at + i - half), :] = source[grain(i), :]

        moved(count, 0, half - at, to_left)
        moved(count, half - at, count, to_right)
        at = at + count


def assemble_kernel(n_seq, table, groups, branch_of, *refs):
    path, sources = refs[-1], refs[:-1]
    half = sources[0].shape[0] // GRAIN
    seq_index = lax.axis_index("seq")
    here = ring_place(seq_index, n_seq)
    path[...] = jnp.zeros_like(path)
    group = groups[0, seq_index]

    def piece(number, carry):
        level = lax.div(number, 3)
        kind = lax.rem(number, 3)
        n = jnp.where(
            level == 0, 0, jnp.where(level == 1, 1 + branch_of[0, group], 1 + BRANCHES + group)
        )
        count = table[4, n]
        first = table[2, n]
        owner = table[1, n]
        before = lax.rem(owner + (n_seq - 1), n_seq)
        after = lax.rem(owner + 1, n_seq)
        to_next = table[8, owner]
        passed = to_next + table[9, owner]
        start = jnp.where(kind == 0, 0, jnp.where(kind == 1, to_next, passed))
        stop = jnp.where(kind == 0, to_next, jnp.where(kind == 1, passed, first + count))
        seat = jnp.where(kind == 0, after, jnp.where(kind == 1, before, owner))
        low = jnp.where(
            kind == 0,
            -table[10, after],
            jnp.where(
                kind == 1,
                to_next - table[10, before] - table[8, lax.rem(before + (n_seq - 1), n_seq)],
                passed,
            ),
        )
        away = lax.rem(here - seat + n_seq, n_seq)
        for k in range(n_seq):

            @pl.when(away == k)
            def _(k=k):
                def put(source, lowest):
                    def copy(i):
                        path[level, grain(i), :] = source[grain(first + i - lowest), :]

                    return copy

                edge = low + half
                moved(
                    count, start - first, jnp.minimum(stop, edge) - first, put(sources[2 * k], low)
                )
                moved(
                    count,
                    jnp.maximum(start, edge) - first,
                    stop - first,
                    put(sources[2 * k + 1], edge),
                )

        return carry

    lax.fori_loop(0, 9, piece, 0)


def attention_kernel(
    n_tensor, order, table, groups, branch_of, buckets, weights, query, key, value, path, out, own, bias
):
    seq_index = lax.axis_index("seq")
    tensor_index = lax.axis_index("tensor")
    rows, width = out.shape
    heads = width // HEAD
    cap = path.shape[1]
    block = rows // n_tensor
    for number, which in enumerate(order):
        seat = lax.bitwise_xor(tensor_index, jnp.int32(which))
        target = pl.ds(pl.multiple_of(seat * block, block), block)
        for place, source in enumerate((query, key, value)):
            own[target, place * width : (place + 1) * width] = source[
                number * block : (number + 1) * block, :
            ]
    group = groups[0, seq_index]
    counts = [table[0, n] for n in (0, 1 + branch_of[0, group], 1 + BRANCHES + group)]
    starts = [jnp.int32(0), counts[0], counts[0] + counts[1]]
    base = counts[0] + counts[1] + counts[2]
    rels = buckets.shape[1]
    bucket = jnp.broadcast_to(buckets[...], (heads, rels))
    reversed_bias = jnp.zeros((heads, rels), jnp.float32)
    for b in range(weights.shape[1]):
        reversed_bias = jnp.where(bucket == b, weights[:, b : b + 1], reversed_bias)
    half = rels // 2
    window = 2 * rows
    for part in range(4):
        shift = (starts[part] - base) if part < 3 else jnp.int32(0)
        turn = half + 1 + shift
        turned = pltpu.roll(reversed_bias, lax.rem(turn + rels, rels), 1)
        bias[part] = jnp.concatenate([turned[:, :rows], turned[:, rels - rows :]], axis=1)
    key_row = iota((cap, 2 * rows), 0)
    half_row = iota((2 * HEAD, rows), 0) < HEAD

    def one_pair(pair, carry):
        def columns(offset):
            return pl.ds(pl.multiple_of(offset + pair * 2 * HEAD, 2 * HEAD), 2 * HEAD)

        query_t = jnp.transpose(own[:, columns(0)].astype(jnp.float32))
        query_t = jnp.concatenate(
            [jnp.where(half_row, query_t, 0.0), jnp.where(half_row, 0.0, query_t)], axis=1
        ).astype(jnp.bfloat16)
        scores = []
        for part in range(4):
            keys = path[part, :, columns(0)] if part < 3 else own[:, columns(width)]
            score = jnp.dot(keys, query_t, preferred_element_type=jnp.float32)
            slabs = []
            for head in range(2):
                line = jnp.broadcast_to(
                    bias[part, pl.ds(2 * pair + head, 1), :], (rows // 2, window)
                )
                rolled = pltpu.roll(line, 0, 1, stride=1, stride_axis=0)
                lower = jnp.concatenate(
                    [rolled[:, window - rows // 2 :], rolled[:, : rows // 2]], axis=1
                )
                slabs.append(jnp.concatenate([rolled[:, :rows], lower], axis=0))
            score = score + jnp.concatenate(slabs, axis=1)
            if part < 3:
                score = jnp.where(key_row < counts[part], score, -1e30)
            scores.append(score)
        peak = jnp.max(scores[0], axis=0, keepdims=True)
        for score in scores[1:]:
            peak = jnp.maximum(peak, jnp.max(score, axis=0, keepdims=True))
        total = jnp.zeros_like(peak)
        summed = jnp.zeros((2 * HEAD, 2 * rows), jnp.float32)
        for part in range(4):
            chance = jnp.exp(scores[part] - peak)
            total = total + jnp.sum(chance, axis=0, keepdims=True)
            values = path[part, :, columns(width)] if part < 3 else own[:, columns(2 * width)]
            summed = summed + lax.dot_general(
                values,
                chance.astype(jnp.bfloat16),
                (((0,), (0,)), ((), ())),
                preferred_element_type=jnp.float32,
            )
        scaled = summed / total
        both = jnp.concatenate([scaled[:HEAD, :rows], scaled[HEAD:, rows:]], axis=0)
        own[:, columns(0)] = jnp.transpose(both).astype(jnp.bfloat16)
        return carry

    lax.fori_loop(0, heads // 2, one_pair, 0)
    for number, which in enumerate(order):
        seat = lax.bitwise_xor(tensor_index, jnp.int32(which))
        out[number * block : (number + 1) * block, :] = own[
            pl.ds(pl.multiple_of(seat * block, block), block), :width
        ]


def vmem(count=1):
    return [pl.BlockSpec(memory_space=pltpu.VMEM)] * count


def smem(count=1):
    return [pl.BlockSpec(memory_space=pltpu.SMEM)] * count


def gather_blocks(own, size, order):
    blocks = {0: own}
    for i in sorted(range(1, size), key=lambda i: (bin(i).count("1"), -i)):
        low = i & -i
        blocks[i] = lax.ppermute(blocks[i ^ low], "tensor", xor_pairs(size, low))
    return jnp.concatenate([blocks[i] for i in order], axis=0)


def scatter_sum(rows, weight, size):
    half = rows.shape[0] // 2
    sent = jnp.dot(rows[:half], weight, preferred_element_type=jnp.float32).astype(jnp.bfloat16)
    arrived = lax.ppermute(sent, "tensor", xor_pairs(size, 1))
    total = jnp.dot(rows[half:], weight, preferred_element_type=jnp.float32)
    total = total + arrived.astype(jnp.float32)
    mask = 2
    while mask < size:
        half //= 2
        arrived = lax.ppermute(total[:half].astype(jnp.bfloat16), "tensor", xor_pairs(size, mask))
        total = total[half:] + arrived.astype(jnp.float32)
        mask *= 2
    return total


def ring_branch(rows, n_seq, cap, table, kept, from_before, from_after, groups, branch_of):
    width = kept.shape[1]
    limit = pltpu.CompilerParams(vmem_limit_bytes=32 * MIB)
    left, right = pl.pallas_call(
        functools.partial(merge_kernel, n_seq),
        grid=(1,),
        out_shape=[jax.ShapeDtypeStruct((rows // 2, width), kept.dtype)] * 2,
        in_specs=smem() + [pl.BlockSpec((rows, width), lambda i: (0, 0))] + vmem(2),
        out_specs=vmem(2),
        compiler_params=limit,
    )(table, kept, from_before, from_after)
    sources = [None] * (2 * n_seq)
    sources[0], sources[1] = left, right
    moving = [[left, right], [left, right]]
    for hop in range(1, n_seq // 2 + 1):
        for way in range(2):
            pairs = ring_pairs(n_seq, 1 if way == 0 else -1)
            for half in range(2):
                if hop == n_seq // 2 and way != half:
                    continue
                moving[way][half] = lax.ppermute(moving[way][half], "seq", pairs)
                away = hop if way == 0 else n_seq - hop
                sources[2 * away + half] = moving[way][half]
    return pl.pallas_call(
        functools.partial(assemble_kernel, n_seq),
        out_shape=jax.ShapeDtypeStruct((3, cap, width), kept.dtype),
        in_specs=smem(3) + vmem(len(sources)),
        out_specs=vmem()[0],
        compiler_params=limit,
    )(table, groups, branch_of, *sources)


def per_device(
    hidden,
    attn_gain,
    attn_query,
    attn_key,
    attn_value,
    attn_out,
    ff_gain,
    ff_gate,
    ff_up,
    ff_down,
    final_gain,
    embedding,
    rel_weight,
    bucket_table,
    prefix_kv,
    node_lengths,
    group_branch,
    node_slot,
    request_group,
):
    n_seq = lax.axis_size("seq")
    n_tensor = lax.axis_size("tensor")
    tensor_index = lax.axis_index("tensor")
    own_rows, width = hidden.shape
    assert request_group.shape[0] == n_seq
    order = block_order(n_tensor)
    slots_here, cap, head_cols = prefix_kv.shape[1:]
    most = slots_here * cap
    classes = [most] + [c for c in CLASSES if c < most]
    passed = min(PASSED, most)
    groups = request_group[None, :]
    branch_of = group_branch[None, :]
    table = pl.pallas_call(
        functools.partial(plan_kernel, n_seq, slots_here, passed, classes),
        out_shape=jax.ShapeDtypeStruct((16, 128), jnp.int32),
        in_specs=vmem(4),
        out_specs=vmem()[0],
    )(node_lengths[None, :], node_slot[None, :], branch_of, groups)
    onward, backward, kept = pl.pallas_call(
        functools.partial(pack_kernel, n_seq, node_lengths.shape[0]),
        out_shape=[
            jax.ShapeDtypeStruct((size, 2 * head_cols), prefix_kv.dtype)
            for size in (passed, passed, most)
        ],
        in_specs=smem() + vmem(),
        out_specs=vmem(3),
        compiler_params=pltpu.CompilerParams(vmem_limit_bytes=32 * MIB),
    )(table, prefix_kv)
    normed = rms_scale(hidden, attn_gain).astype(jnp.bfloat16)
    normed, onward, backward = lax.optimization_barrier((normed, onward, backward))
    from_before = lax.ppermute(onward, "seq", ring_pairs(n_seq, 1))
    from_after = lax.ppermute(backward, "seq", ring_pairs(n_seq, -1))
    rows = gather_blocks(normed, n_tensor, order)
    projected = [
        jnp.dot(rows, weight, preferred_element_type=jnp.float32).astype(jnp.bfloat16)
        for weight in (attn_query, attn_key, attn_value)
    ]
    path = lax.switch(
        table[11, 0],
        [functools.partial(ring_branch, c, n_seq, cap) for c in classes],
        table,
        kept,
        from_before,
        from_after,
        groups,
        branch_of,
    )
    n_rows = rows.shape[0]
    attn = pl.pallas_call(
        functools.partial(attention_kernel, n_tensor, order),
        out_shape=jax.ShapeDtypeStruct((n_rows, head_cols), jnp.bfloat16),
        in_specs=smem(3) + vmem(6),
        out_specs=vmem()[0],
        scratch_shapes=[
            pltpu.VMEM((n_rows, 3 * head_cols), jnp.bfloat16),
            pltpu.VMEM((4, head_cols // HEAD, 2 * n_rows), jnp.float32),
        ],
        compiler_params=pltpu.CompilerParams(vmem_limit_bytes=32 * MIB),
    )(
        table,
        groups,
        branch_of,
        bucket_table[::-1][None, :],
        jnp.transpose(rel_weight),
        *projected,
        path,
    )
    attn_sum = scatter_sum(attn, attn_out, n_tensor)
    mid = (hidden.astype(jnp.float32) + attn_sum).astype(jnp.bfloat16)
    rows = gather_blocks(rms_scale(mid, ff_gain).astype(jnp.bfloat16), n_tensor, order)
    gate_part = jnp.dot(rows, ff_gate, preferred_element_type=jnp.float32)
    up_part = jnp.dot(rows, ff_up, preferred_element_type=jnp.float32)
    inner = (jax.nn.gelu(gate_part, approximate=True) * up_part).astype(jnp.bfloat16)
    ff_summed = scatter_sum(inner, ff_down, n_tensor)
    hidden_out = (mid.astype(jnp.float32) + ff_summed).astype(jnp.bfloat16)
    last = hidden_out[own_rows - 1 :]
    copies = [
        lax.ppermute(last, "tensor", [(n_tensor - 1, i)]) for i in range(n_tensor - 1)
    ]
    last = jnp.where(tensor_index == n_tensor - 1, last, sum(copies[1:], copies[0]))
    seq_index = lax.axis_index("seq")
    shifted = [last] + [
        lax.ppermute(last, "seq", [(i, (i + k) % n_seq) for i in range(n_seq)])
        for k in range(1, n_seq)
    ]
    stacked = jnp.concatenate(shifted, axis=0)
    from_row = lax.rem(seq_index - jnp.arange(n_seq) + n_seq, n_seq)
    last_rows = stacked[from_row].astype(jnp.float32)
    mean_square = jnp.mean(last_rows * last_rows, axis=1)
    last_rms = jnp.sqrt(mean_square)
    final_rows = (last_rows * lax.rsqrt(mean_square + 1e-06)[:, None] * final_gain).astype(
        jnp.bfloat16
    )
    embed_cols = embedding.shape[1]
    columns = lax.dynamic_slice_in_dim(final_rows, tensor_index * embed_cols, embed_cols, 1)
    logits = lax.dot_general(
        columns, embedding, (((1,), (1,)), ((), ())), preferred_element_type=jnp.float32
    )
    mask = 1
    while mask < n_tensor:
        sent = logits.astype(jnp.bfloat16)
        arrived = lax.ppermute(sent, "tensor", xor_pairs(n_tensor, mask))
        logits = sent.astype(jnp.float32) + arrived.astype(jnp.float32)
        mask *= 2
    top = jnp.max(logits, axis=1)
    tops = [top] + [
        lax.ppermute(top, "seq", [(i, (i + k) % n_seq) for i in range(n_seq)])
        for k in range(1, n_seq)
    ]
    top_logit = functools.reduce(jnp.maximum, tops)
    return (hidden_out, last_rms, top_logit)


def solution(mesh):
    return jax.shard_map(
        per_device,
        mesh=mesh,
        in_specs=(
            P(("seq", "tensor"), None),
            P(),
            P(None, "tensor"),
            P(None, "tensor"),
            P(None, "tensor"),
            P("tensor", None),
            P(),
            P(None, "tensor"),
            P(None, "tensor"),
            P("tensor", None),
            P(),
            P("seq", "tensor"),
            P(None, "tensor"),
            P(),
            P(None, "seq", None, "tensor"),
            P(),
            P(),
            P(),
            P(),
        ),
        out_specs=(P(("seq", "tensor"), None), P(), P()),
        check_vma=False,
    )
```

```python
import functools

import jax
import jax.numpy as jnp
from jax import lax
from jax.experimental import pallas as pl
from jax.experimental.pallas import tpu as pltpu
from jax.sharding import PartitionSpec as P

BRANCHES = 7
HEAD = 64
GRAIN = 16
MIB = 1 << 20
PASSED = 160
CLASSES = (448, 320, 256, 224, 192, 160)


def rms_scale(values, gain):
    widened = values.astype(jnp.float32)
    mean_square = jnp.mean(widened * widened, axis=-1, keepdims=True)
    return widened * lax.rsqrt(mean_square + 1e-06) * gain


def gated(rows, gate, up):
    gate_part = jnp.dot(rows, gate, preferred_element_type=jnp.float32)
    up_part = jnp.dot(rows, up, preferred_element_type=jnp.float32)
    return (jax.nn.gelu(gate_part, approximate=True) * up_part).astype(jnp.bfloat16)


def xor_pairs(size, mask):
    return [(i, i ^ mask) for i in range(size)]


def ring_place(index, size):
    half = lax.shift_right_logical(index, jnp.int32(1))
    return jnp.where(lax.bitwise_and(index, jnp.int32(1)) == 0, half, size - 1 - half)


def ring_pairs(size, step):
    order = list(range(0, size, 2)) + list(range(1, size, 2))[::-1]
    return [(order[i], order[(i + step) % size]) for i in range(size)]


def block_order(size):
    bits = size.bit_length() - 1
    return sorted(range(size), key=lambda i: -int(format(i, "b").zfill(bits)[::-1], 2))


def iota(shape, axis):
    return lax.broadcasted_iota(jnp.int32, shape, axis)


def plan_kernel(n_seq, slots_here, passed, classes, lengths, slots, branch_of, groups, table):
    nodes = lengths.shape[1]
    requests = groups.shape[1]
    eye = iota((nodes, nodes), 0) == iota((nodes, nodes), 1)
    seq_eye = iota((n_seq, n_seq), 0) == iota((n_seq, n_seq), 1)

    def column(row):
        return jnp.sum(jnp.where(eye, row, 0), axis=1, keepdims=True)

    def seq_row(col):
        return jnp.sum(jnp.where(seq_eye, col, 0), axis=0, keepdims=True)

    slot = slots[...]
    owner = jnp.zeros_like(slot)
    for k in range(1, n_seq):
        owner = owner + (slot >= k * slots_here).astype(jnp.int32)
    place = ring_place(owner, n_seq)
    req_eye = iota((requests, requests), 0) == iota((requests, requests), 1)
    group = jnp.sum(jnp.where(req_eye, groups[...], 0), axis=1, keepdims=True)
    n_groups = branch_of.shape[1]
    branch = jnp.sum(
        jnp.where(iota((requests, n_groups), 1) == group, branch_of[...], 0), axis=1, keepdims=True
    )
    node = iota((requests, nodes), 1)
    need = (node == 0) | (node == 1 + branch) | (node == 1 + BRANCHES + group)
    needed = jnp.max(need.astype(jnp.int32), axis=0, keepdims=True)
    grains = needed * lax.shift_right_logical(lengths[...] + (GRAIN - 1), jnp.int32(4))
    earlier = iota((nodes, nodes), 0) < iota((nodes, nodes), 1)
    before = (column(place) == place) & earlier
    first = jnp.sum(jnp.where(before, column(grains), 0), axis=0, keepdims=True)
    held = jnp.sum(
        jnp.where(iota((n_seq, nodes), 0) == place, grains, 0), axis=1, keepdims=True
    )
    every = jnp.sum(held, axis=0, keepdims=True)
    upto = iota((n_seq, n_seq), 1) <= iota((n_seq, n_seq), 0)
    surplus = n_seq * seq_row(held) - every
    running = jnp.sum(jnp.where(upto, surplus, 0), axis=1, keepdims=True)
    middle = lax.shift_right_arithmetic(
        jnp.max(running, axis=0, keepdims=True) + jnp.min(running, axis=0, keepdims=True),
        jnp.int32(1),
    )
    flow = lax.shift_right_arithmetic(
        running - middle + n_seq // 2, jnp.int32(n_seq.bit_length() - 1)
    )
    most = passed // GRAIN
    flow = jnp.minimum(jnp.maximum(flow, -most), most)
    before_me = iota((n_seq, n_seq), 1) == lax.rem(
        iota((n_seq, n_seq), 0) + (n_seq - 1), jnp.int32(n_seq)
    )
    after_me = iota((n_seq, n_seq), 1) == lax.rem(
        iota((n_seq, n_seq), 0) + 1, jnp.int32(n_seq)
    )

    def from_seat(which, col):
        return jnp.sum(jnp.where(which, seq_row(col), 0), axis=1, keepdims=True)

    onward = jnp.minimum(jnp.maximum(flow, 0), held)
    backward = jnp.minimum(jnp.maximum(-from_seat(before_me, flow), 0), held - onward)
    kept = held - onward - backward
    block = kept + from_seat(before_me, onward) + from_seat(after_me, backward)
    largest = jnp.max(block, axis=0, keepdims=True) * GRAIN
    choice = jnp.zeros((1, 1), jnp.int32)
    for number, rows in enumerate(classes):
        choice = jnp.where(largest <= rows, number, choice)
    table[...] = jnp.zeros_like(table)
    for number, row in enumerate((lengths[...], place, first, slot - owner * slots_here, grains)):
        table[number : number + 1, :nodes] = row
    for number, col in enumerate((onward, backward, kept)):
        table[8 + number : 9 + number, :n_seq] = seq_row(col)
    table[11:12, :] = jnp.broadcast_to(choice, (1, table.shape[1]))


def moved(count, start, stop, copy):
    def step(i, carry):
        copy(i)
        return carry

    lax.fori_loop(jnp.maximum(start, 0), jnp.minimum(stop, count), step, 0)


def grain(i):
    return pl.ds(pl.multiple_of(i * GRAIN, GRAIN), GRAIN)


def pack_kernel(n_seq, nodes, table, cache, onward, backward, kept):
    here = ring_place(lax.axis_index("seq"), n_seq)
    width = cache.shape[3]
    to_next = table[8, here]
    passed = to_next + table[9, here]

    def one_node(n, carry):
        @pl.when((table[1, n] == here) & (table[4, n] > 0))
        def _():
            slot = table[3, n]
            count = table[4, n]
            first = table[2, n]

            def put(target, low):
                def copy(i):
                    target[grain(first + i - low), :width] = cache[0, slot, grain(i), :]
                    target[grain(first + i - low), width:] = cache[1, slot, grain(i), :]

                return copy

            moved(count, 0, to_next - first, put(onward, 0))
            moved(count, to_next - first, passed - first, put(backward, to_next))
            moved(count, passed - first, count, put(kept, passed))

        return carry

    lax.fori_loop(0, nodes, one_node, 0)


def merge_kernel(n_seq, table, kept, from_before, from_after, left, right):
    here = ring_place(lax.axis_index("seq"), n_seq)
    before = lax.rem(here + (n_seq - 1), n_seq)
    after = lax.rem(here + 1, n_seq)
    half = left.shape[0] // GRAIN
    left[...] = kept[: left.shape[0], :]
    right[...] = kept[left.shape[0] :, :]
    at = table[10, here]
    for source, count in ((from_before, table[8, before]), (from_after, table[9, after])):

        def to_left(i, source=source, at=at):
            left[grain(at + i), :] = source[grain(i), :]

        def to_right(i, source=source, at=at):
            right[grain(at + i - half), :] = source[grain(i), :]

        moved(count, 0, half - at, to_left)
        moved(count, half - at, count, to_right)
        at = at + count


def assemble_kernel(n_seq, table, groups, branch_of, *refs):
    path, sources = refs[-1], refs[:-1]
    half = sources[0].shape[0] // GRAIN
    seq_index = lax.axis_index("seq")
    here = ring_place(seq_index, n_seq)
    path[...] = jnp.zeros_like(path)
    group = groups[0, seq_index]

    def piece(number, carry):
        level = lax.div(number, 3)
        kind = lax.rem(number, 3)
        n = jnp.where(
            level == 0, 0, jnp.where(level == 1, 1 + branch_of[0, group], 1 + BRANCHES + group)
        )
        count = table[4, n]
        first = table[2, n]
        owner = table[1, n]
        before = lax.rem(owner + (n_seq - 1), n_seq)
        after = lax.rem(owner + 1, n_seq)
        to_next = table[8, owner]
        passed = to_next + table[9, owner]
        start = jnp.where(kind == 0, 0, jnp.where(kind == 1, to_next, passed))
        stop = jnp.where(kind == 0, to_next, jnp.where(kind == 1, passed, first + count))
        seat = jnp.where(kind == 0, after, jnp.where(kind == 1, before, owner))
        low = jnp.where(
            kind == 0,
            -table[10, after],
            jnp.where(
                kind == 1,
                to_next - table[10, before] - table[8, lax.rem(before + (n_seq - 1), n_seq)],
                passed,
            ),
        )
        away = lax.rem(here - seat + n_seq, n_seq)
        for k in range(n_seq):

            @pl.when(away == k)
            def _(k=k):
                def put(source, lowest):
                    def copy(i):
                        path[level, grain(i), :] = source[grain(first + i - lowest), :]

                    return copy

                edge = low + half
                moved(
                    count, start - first, jnp.minimum(stop, edge) - first, put(sources[2 * k], low)
                )
                moved(
                    count,
                    jnp.maximum(start, edge) - first,
                    stop - first,
                    put(sources[2 * k + 1], edge),
                )

        return carry

    lax.fori_loop(0, 9, piece, 0)


def attention_kernel(
    n_tensor, order, table, groups, branch_of, buckets, weights, query, key, value, path, out, end, own, bias
):
    seq_index = lax.axis_index("seq")
    tensor_index = lax.axis_index("tensor")
    rows, width = out.shape
    heads = width // HEAD
    cap = path.shape[1]
    block = rows // n_tensor
    for number, which in enumerate(order):
        seat = lax.bitwise_xor(tensor_index, jnp.int32(which))
        target = pl.ds(pl.multiple_of(seat * block, block), block)
        for place, source in enumerate((query, key, value)):
            own[target, place * width : (place + 1) * width] = source[
                number * block : (number + 1) * block, :
            ]
    group = groups[0, seq_index]
    counts = [table[0, n] for n in (0, 1 + branch_of[0, group], 1 + BRANCHES + group)]
    starts = [jnp.int32(0), counts[0], counts[0] + counts[1]]
    base = counts[0] + counts[1] + counts[2]
    rels = buckets.shape[1]
    bucket = jnp.broadcast_to(buckets[...], (heads, rels))
    reversed_bias = jnp.zeros((heads, rels), jnp.float32)
    for b in range(weights.shape[1]):
        reversed_bias = jnp.where(bucket == b, weights[:, b : b + 1], reversed_bias)
    half = rels // 2
    window = 2 * rows
    for part in range(4):
        shift = (starts[part] - base) if part < 3 else jnp.int32(0)
        turn = half + 1 + shift
        turned = pltpu.roll(reversed_bias, lax.rem(turn + rels, rels), 1)
        bias[part] = jnp.concatenate([turned[:, :rows], turned[:, rels - rows :]], axis=1)
    key_row = iota((cap, 2 * rows), 0)
    half_row = iota((2 * HEAD, rows), 0) < HEAD

    def one_pair(pair, carry):
        def columns(offset):
            return pl.ds(pl.multiple_of(offset + pair * 2 * HEAD, 2 * HEAD), 2 * HEAD)

        query_t = jnp.transpose(own[:, columns(0)].astype(jnp.float32))
        query_t = jnp.concatenate(
            [jnp.where(half_row, query_t, 0.0), jnp.where(half_row, 0.0, query_t)], axis=1
        ).astype(jnp.bfloat16)
        scores = []
        for part in range(4):
            keys = path[part, :, columns(0)] if part < 3 else own[:, columns(width)]
            score = jnp.dot(keys, query_t, preferred_element_type=jnp.float32)
            slabs = []
            for head in range(2):
                line = jnp.broadcast_to(
                    bias[part, pl.ds(2 * pair + head, 1), :], (rows // 2, window)
                )
                rolled = pltpu.roll(line, 0, 1, stride=1, stride_axis=0)
                lower = jnp.concatenate(
                    [rolled[:, window - rows // 2 :], rolled[:, : rows // 2]], axis=1
                )
                slabs.append(jnp.concatenate([rolled[:, :rows], lower], axis=0))
            score = score + jnp.concatenate(slabs, axis=1)
            if part < 3:
                score = jnp.where(key_row < counts[part], score, -1e30)
            scores.append(score)
        peak = jnp.max(scores[0], axis=0, keepdims=True)
        for score in scores[1:]:
            peak = jnp.maximum(peak, jnp.max(score, axis=0, keepdims=True))
        total = jnp.zeros_like(peak)
        summed = jnp.zeros((2 * HEAD, 2 * rows), jnp.float32)
        for part in range(4):
            chance = jnp.exp(scores[part] - peak)
            total = total + jnp.sum(chance, axis=0, keepdims=True)
            values = path[part, :, columns(width)] if part < 3 else own[:, columns(2 * width)]
            summed = summed + lax.dot_general(
                values,
                chance.astype(jnp.bfloat16),
                (((0,), (0,)), ((), ())),
                preferred_element_type=jnp.float32,
            )
        scaled = summed / total
        both = jnp.concatenate([scaled[:HEAD, :rows], scaled[HEAD:, rows:]], axis=0)
        own[:, columns(0)] = jnp.transpose(both).astype(jnp.bfloat16)
        return carry

    lax.fori_loop(0, heads // 2, one_pair, 0)
    for number, which in enumerate(order):
        seat = lax.bitwise_xor(tensor_index, jnp.int32(which))
        out[number * block : (number + 1) * block, :] = own[
            pl.ds(pl.multiple_of(seat * block, block), block), :width
        ]
    end[...] = own[rows - GRAIN :, :width]


def vmem(count=1):
    return [pl.BlockSpec(memory_space=pltpu.VMEM)] * count


def smem(count=1):
    return [pl.BlockSpec(memory_space=pltpu.SMEM)] * count


def gather_blocks(own, size, order):
    blocks = {0: own}
    for i in sorted(range(1, size), key=lambda i: (bin(i).count("1"), -i)):
        low = i & -i
        blocks[i] = lax.ppermute(blocks[i ^ low], "tensor", xor_pairs(size, low))
    return [blocks[i] for i in order]


def seq_fold(value, size, join):
    value = join([value, lax.ppermute(value, "seq", xor_pairs(size, 1))])
    return join(
        [value] + [lax.ppermute(value, "seq", xor_pairs(size, i)) for i in range(2, size, 2)]
    )


def tensor_sum(value, size, kind):
    mask = 1
    while mask < size:
        sent = value.astype(kind)
        arrived = lax.ppermute(sent, "tensor", xor_pairs(size, mask))
        value = sent.astype(jnp.float32) + arrived.astype(jnp.float32)
        mask *= 2
    return value


def scatter_sum(sent, held, added, size):
    block = 2 * held.shape[0] // size
    arrived = lax.ppermute(sent, "tensor", xor_pairs(size, 1))
    sums = added + held[-block:] + arrived[-block:].astype(jnp.float32)
    total = held[:-block] + arrived[:-block].astype(jnp.float32)
    mask = 2
    while mask < size:
        count = total.shape[0] // block + 1
        first = total[: count // 2 * block].astype(jnp.bfloat16)
        arrived = lax.ppermute(first, "tensor", xor_pairs(size, mask))
        sums = sums + arrived[-block:].astype(jnp.float32)
        total = total[count // 2 * block :] + arrived[:-block].astype(jnp.float32)
        mask *= 2
    return sums


def logits_kernel(rows, words, out):
    out[...] = lax.dot_general(
        rows[...], words[...], (((1,), (1,)), ((), ())), preferred_element_type=jnp.float32
    )


def ring_branch(
    rows, n_seq, n_tensor, cap, table, kept, from_before, from_after, groups, branch_of, hidden, gain, weights
):
    width = kept.shape[1]
    limit = pltpu.CompilerParams(vmem_limit_bytes=32 * MIB)
    left, right = pl.pallas_call(
        functools.partial(merge_kernel, n_seq),
        grid=(1,),
        out_shape=[jax.ShapeDtypeStruct((rows // 2, width), kept.dtype)] * 2,
        in_specs=smem() + [pl.BlockSpec((rows, width), lambda i: (0, 0))] + vmem(2),
        out_specs=vmem(2),
        compiler_params=limit,
    )(table, kept, from_before, from_after)
    sources = [None] * (2 * n_seq)
    sources[0], sources[1] = left, right
    moving = [[left, right], [left, right]]
    for hop in range(1, n_seq // 2 + 1):
        for way in range(2):
            pairs = ring_pairs(n_seq, 1 if way == 0 else -1)
            for half in range(2):
                if hop == n_seq // 2 and way != half:
                    continue
                moving[way][half] = lax.ppermute(moving[way][half], "seq", pairs)
                away = hop if way == 0 else n_seq - hop
                sources[2 * away + half] = moving[way][half]
    normed = rms_scale(hidden, gain).astype(jnp.bfloat16)
    normed = jnp.concatenate(gather_blocks(normed, n_tensor, block_order(n_tensor)), axis=0)
    projected = [
        jnp.dot(normed, weight, preferred_element_type=jnp.float32).astype(jnp.bfloat16)
        for weight in weights
    ]
    path = pl.pallas_call(
        functools.partial(assemble_kernel, n_seq),
        out_shape=jax.ShapeDtypeStruct((3, cap, width), kept.dtype),
        in_specs=smem(3) + vmem(len(sources)),
        out_specs=vmem()[0],
        compiler_params=limit,
    )(table, groups, branch_of, *sources)
    return (path, *projected)


def per_device(
    hidden,
    attn_gain,
    attn_query,
    attn_key,
    attn_value,
    attn_out,
    ff_gain,
    ff_gate,
    ff_up,
    ff_down,
    final_gain,
    embedding,
    rel_weight,
    bucket_table,
    prefix_kv,
    node_lengths,
    group_branch,
    node_slot,
    request_group,
):
    n_seq = lax.axis_size("seq")
    n_tensor = lax.axis_size("tensor")
    tensor_index = lax.axis_index("tensor")
    own_rows, width = hidden.shape
    assert request_group.shape[0] == n_seq
    order = block_order(n_tensor)
    slots_here, cap, head_cols = prefix_kv.shape[1:]
    most = slots_here * cap
    classes = [most] + [c for c in CLASSES if c < most]
    passed = min(PASSED, most)
    groups = request_group[None, :]
    branch_of = group_branch[None, :]
    table = pl.pallas_call(
        functools.partial(plan_kernel, n_seq, slots_here, passed, classes),
        out_shape=jax.ShapeDtypeStruct((16, 128), jnp.int32),
        in_specs=vmem(4),
        out_specs=vmem()[0],
    )(node_lengths[None, :], node_slot[None, :], branch_of, groups)
    onward, backward, kept = pl.pallas_call(
        functools.partial(pack_kernel, n_seq, node_lengths.shape[0]),
        out_shape=[
            jax.ShapeDtypeStruct((size, 2 * head_cols), prefix_kv.dtype)
            for size in (passed, passed, most)
        ],
        in_specs=smem() + vmem(),
        out_specs=vmem(3),
        compiler_params=pltpu.CompilerParams(vmem_limit_bytes=32 * MIB),
    )(table, prefix_kv)
    from_before = lax.ppermute(onward, "seq", ring_pairs(n_seq, 1))
    from_after = lax.ppermute(backward, "seq", ring_pairs(n_seq, -1))
    path, *projected = lax.switch(
        table[11, 0],
        [functools.partial(ring_branch, c, n_seq, n_tensor, cap) for c in classes],
        table,
        kept,
        from_before,
        from_after,
        groups,
        branch_of,
        hidden,
        attn_gain,
        (attn_query, attn_key, attn_value),
    )
    n_rows = own_rows * n_tensor
    attn, attn_end = pl.pallas_call(
        functools.partial(attention_kernel, n_tensor, order),
        out_shape=[
            jax.ShapeDtypeStruct((size, head_cols), jnp.bfloat16) for size in (n_rows, GRAIN)
        ],
        in_specs=smem(3) + vmem(6),
        out_specs=vmem(2),
        scratch_shapes=[
            pltpu.VMEM((n_rows, 3 * head_cols), jnp.bfloat16),
            pltpu.VMEM((4, head_cols // HEAD, 2 * n_rows), jnp.float32),
        ],
        compiler_params=pltpu.CompilerParams(vmem_limit_bytes=32 * MIB),
    )(
        table,
        groups,
        branch_of,
        bucket_table[::-1][None, :],
        jnp.transpose(rel_weight),
        *projected,
        path,
    )
    half = n_rows // 2
    sent = jnp.dot(attn[:half], attn_out, preferred_element_type=jnp.float32).astype(jnp.bfloat16)
    held = jnp.dot(attn[half:], attn_out, preferred_element_type=jnp.float32)
    keeper = tensor_index == n_tensor - 1
    ends = jnp.concatenate([attn_end[GRAIN - 1 :], hidden[own_rows - 1 :]], axis=1)
    ends, sent = lax.optimization_barrier((ends, sent))
    ends = seq_fold(ends, n_seq, functools.partial(jnp.concatenate, axis=0))
    mid = scatter_sum(sent, held, hidden.astype(jnp.float32), n_tensor).astype(jnp.bfloat16)
    mid_normed = rms_scale(mid, ff_gain).astype(jnp.bfloat16)
    ends, mid_normed = lax.optimization_barrier((ends, mid_normed))
    ends = ends[lax.bitwise_xor(lax.axis_index("seq"), jnp.arange(n_seq))]
    part = jnp.dot(ends[:, :head_cols], attn_out, preferred_element_type=jnp.float32)
    part = part + jnp.where(keeper, ends[:, head_cols:].astype(jnp.float32), 0.0)
    end_mid = tensor_sum(part, n_tensor, jnp.float32).astype(jnp.bfloat16)
    end_normed = rms_scale(end_mid, ff_gain).astype(jnp.bfloat16)
    end_normed = jnp.pad(end_normed, ((0, -n_seq % GRAIN), (0, 0)))
    blocks = gather_blocks(mid_normed, n_tensor, order)
    blocks = blocks[: n_tensor // 2] + [end_normed] + blocks[n_tensor // 2 :]
    inner = gated(jnp.concatenate(blocks, axis=0), ff_gate, ff_up)
    sent = jnp.dot(inner[:half], ff_down, preferred_element_type=jnp.float32).astype(jnp.bfloat16)
    part = jnp.dot(inner[half:-half], ff_down, preferred_element_type=jnp.float32)[:n_seq]
    held = jnp.dot(inner[-half:], ff_down, preferred_element_type=jnp.float32)
    sent, part, held = lax.optimization_barrier((sent, part, held))
    end_out = end_mid.astype(jnp.float32) + tensor_sum(part, n_tensor, jnp.bfloat16)
    hidden_out = scatter_sum(sent, held, mid.astype(jnp.float32), n_tensor).astype(jnp.bfloat16)
    last_rows = end_out.astype(jnp.bfloat16).astype(jnp.float32)
    mean_square = jnp.mean(last_rows * last_rows, axis=1)
    last_rms = jnp.sqrt(mean_square)
    final_rows = (last_rows * lax.rsqrt(mean_square + 1e-06)[:, None] * final_gain).astype(
        jnp.bfloat16
    )
    embed_cols = embedding.shape[1]
    columns = lax.dynamic_slice_in_dim(final_rows, tensor_index * embed_cols, embed_cols, 1)
    logits = pl.pallas_call(
        logits_kernel,
        out_shape=jax.ShapeDtypeStruct((n_seq, embedding.shape[0]), jnp.float32),
        in_specs=vmem(2),
        out_specs=vmem()[0],
        compiler_params=pltpu.CompilerParams(vmem_limit_bytes=12 * MIB),
    )(columns, embedding)
    top = jnp.max(tensor_sum(logits, n_tensor, jnp.bfloat16), axis=1)
    top_logit = seq_fold(top, n_seq, functools.partial(functools.reduce, jnp.maximum))
    return (hidden_out, last_rms, top_logit)


def solution(mesh):
    return jax.shard_map(
        per_device,
        mesh=mesh,
        in_specs=(
            P(("seq", "tensor"), None),
            P(),
            P(None, "tensor"),
            P(None, "tensor"),
            P(None, "tensor"),
            P("tensor", None),
            P(),
            P(None, "tensor"),
            P(None, "tensor"),
            P("tensor", None),
            P(),
            P("seq", "tensor"),
            P(None, "tensor"),
            P(),
            P(None, "seq", None, "tensor"),
            P(),
            P(),
            P(),
            P(),
        ),
        out_specs=(P(("seq", "tensor"), None), P(), P()),
        check_vma=False,
    )
```

```python
import functools

import jax
import jax.numpy as jnp
from jax import lax
from jax.experimental import pallas as pl
from jax.experimental.pallas import tpu as pltpu
from jax.sharding import PartitionSpec as P

BRANCHES = 7
HEAD = 64
GRAIN = 16
MIB = 1 << 20
PASSED = 160
CLASSES = (448, 320, 256, 224, 192, 160)


def rms_scale(values, gain):
    widened = values.astype(jnp.float32)
    mean_square = jnp.mean(widened * widened, axis=-1, keepdims=True)
    return widened * lax.rsqrt(mean_square + 1e-06) * gain


def gated(rows, gate, up):
    gate_part = jnp.dot(rows, gate, preferred_element_type=jnp.float32)
    up_part = jnp.dot(rows, up, preferred_element_type=jnp.float32)
    return (jax.nn.gelu(gate_part, approximate=True) * up_part).astype(jnp.bfloat16)


def xor_pairs(size, mask):
    return [(i, i ^ mask) for i in range(size)]


def ring_place(index, size):
    half = lax.shift_right_logical(index, jnp.int32(1))
    return jnp.where(lax.bitwise_and(index, jnp.int32(1)) == 0, half, size - 1 - half)


def ring_pairs(size, step):
    order = list(range(0, size, 2)) + list(range(1, size, 2))[::-1]
    return [(order[i], order[(i + step) % size]) for i in range(size)]


def block_order(size):
    bits = size.bit_length() - 1
    return sorted(range(size), key=lambda i: -int(format(i, "b").zfill(bits)[::-1], 2))


def iota(shape, axis):
    return lax.broadcasted_iota(jnp.int32, shape, axis)


def plan_kernel(n_seq, slots_here, passed, classes, lengths, slots, branch_of, groups, table):
    nodes = lengths.shape[1]
    requests = groups.shape[1]
    eye = iota((nodes, nodes), 0) == iota((nodes, nodes), 1)
    seq_eye = iota((n_seq, n_seq), 0) == iota((n_seq, n_seq), 1)

    def column(row):
        return jnp.sum(jnp.where(eye, row, 0), axis=1, keepdims=True)

    def seq_row(col):
        return jnp.sum(jnp.where(seq_eye, col, 0), axis=0, keepdims=True)

    slot = slots[...]
    owner = jnp.zeros_like(slot)
    for k in range(1, n_seq):
        owner = owner + (slot >= k * slots_here).astype(jnp.int32)
    place = ring_place(owner, n_seq)
    req_eye = iota((requests, requests), 0) == iota((requests, requests), 1)
    group = jnp.sum(jnp.where(req_eye, groups[...], 0), axis=1, keepdims=True)
    n_groups = branch_of.shape[1]
    branch = jnp.sum(
        jnp.where(iota((requests, n_groups), 1) == group, branch_of[...], 0), axis=1, keepdims=True
    )
    node = iota((requests, nodes), 1)
    need = (node == 0) | (node == 1 + branch) | (node == 1 + BRANCHES + group)
    needed = jnp.max(need.astype(jnp.int32), axis=0, keepdims=True)
    grains = needed * lax.shift_right_logical(lengths[...] + (GRAIN - 1), jnp.int32(4))
    earlier = iota((nodes, nodes), 0) < iota((nodes, nodes), 1)
    before = (column(place) == place) & earlier
    first = jnp.sum(jnp.where(before, column(grains), 0), axis=0, keepdims=True)
    held = jnp.sum(
        jnp.where(iota((n_seq, nodes), 0) == place, grains, 0), axis=1, keepdims=True
    )
    every = jnp.sum(held, axis=0, keepdims=True)
    upto = iota((n_seq, n_seq), 1) <= iota((n_seq, n_seq), 0)
    surplus = n_seq * seq_row(held) - every
    running = jnp.sum(jnp.where(upto, surplus, 0), axis=1, keepdims=True)
    middle = lax.shift_right_arithmetic(
        jnp.max(running, axis=0, keepdims=True) + jnp.min(running, axis=0, keepdims=True),
        jnp.int32(1),
    )
    flow = lax.shift_right_arithmetic(
        running - middle + n_seq // 2, jnp.int32(n_seq.bit_length() - 1)
    )
    most = passed // GRAIN
    flow = jnp.minimum(jnp.maximum(flow, -most), most)
    before_me = iota((n_seq, n_seq), 1) == lax.rem(
        iota((n_seq, n_seq), 0) + (n_seq - 1), jnp.int32(n_seq)
    )
    after_me = iota((n_seq, n_seq), 1) == lax.rem(
        iota((n_seq, n_seq), 0) + 1, jnp.int32(n_seq)
    )

    def from_seat(which, col):
        return jnp.sum(jnp.where(which, seq_row(col), 0), axis=1, keepdims=True)

    onward = jnp.minimum(jnp.maximum(flow, 0), held)
    backward = jnp.minimum(jnp.maximum(-from_seat(before_me, flow), 0), held - onward)
    kept = held - onward - backward
    block = kept + from_seat(before_me, onward) + from_seat(after_me, backward)
    largest = jnp.max(block, axis=0, keepdims=True) * GRAIN
    choice = jnp.zeros((1, 1), jnp.int32)
    for number, rows in enumerate(classes):
        choice = jnp.where(largest <= rows, number, choice)
    table[...] = jnp.zeros_like(table)
    for number, row in enumerate((lengths[...], place, first, slot - owner * slots_here, grains)):
        table[number : number + 1, :nodes] = row
    for number, col in enumerate((onward, backward, kept)):
        table[8 + number : 9 + number, :n_seq] = seq_row(col)
    table[11:12, :] = jnp.broadcast_to(choice, (1, table.shape[1]))


def moved(count, start, stop, copy):
    def step(i, carry):
        copy(i)
        return carry

    lax.fori_loop(jnp.maximum(start, 0), jnp.minimum(stop, count), step, 0)


def grain(i):
    return pl.ds(pl.multiple_of(i * GRAIN, GRAIN), GRAIN)


def pack_kernel(n_seq, nodes, table, cache, onward, backward, kept):
    here = ring_place(lax.axis_index("seq"), n_seq)
    width = cache.shape[3]
    to_next = table[8, here]
    passed = to_next + table[9, here]

    def one_node(n, carry):
        @pl.when((table[1, n] == here) & (table[4, n] > 0))
        def _():
            slot = table[3, n]
            count = table[4, n]
            first = table[2, n]

            def put(target, low):
                def copy(i):
                    target[grain(first + i - low), :width] = cache[0, slot, grain(i), :]
                    target[grain(first + i - low), width:] = cache[1, slot, grain(i), :]

                return copy

            moved(count, 0, to_next - first, put(onward, 0))
            moved(count, to_next - first, passed - first, put(backward, to_next))
            moved(count, passed - first, count, put(kept, passed))

        return carry

    lax.fori_loop(0, nodes, one_node, 0)


def merge_kernel(n_seq, table, kept, from_before, from_after, left, right):
    here = ring_place(lax.axis_index("seq"), n_seq)
    before = lax.rem(here + (n_seq - 1), n_seq)
    after = lax.rem(here + 1, n_seq)
    half = left.shape[0] // GRAIN
    left[...] = kept[: left.shape[0], :]
    right[...] = kept[left.shape[0] :, :]
    at = table[10, here]
    for source, count in ((from_before, table[8, before]), (from_after, table[9, after])):

        def to_left(i, source=source, at=at):
            left[grain(at + i), :] = source[grain(i), :]

        def to_right(i, source=source, at=at):
            right[grain(at + i - half), :] = source[grain(i), :]

        moved(count, 0, half - at, to_left)
        moved(count, half - at, count, to_right)
        at = at + count


def assemble_kernel(n_seq, table, groups, branch_of, *refs):
    path, sources = refs[-1], refs[:-1]
    half = sources[0].shape[0] // GRAIN
    seq_index = lax.axis_index("seq")
    here = ring_place(seq_index, n_seq)
    path[...] = jnp.zeros_like(path)
    group = groups[0, seq_index]

    def piece(number, carry):
        level = lax.div(number, 3)
        kind = lax.rem(number, 3)
        n = jnp.where(
            level == 0, 0, jnp.where(level == 1, 1 + branch_of[0, group], 1 + BRANCHES + group)
        )
        count = table[4, n]
        first = table[2, n]
        owner = table[1, n]
        before = lax.rem(owner + (n_seq - 1), n_seq)
        after = lax.rem(owner + 1, n_seq)
        to_next = table[8, owner]
        passed = to_next + table[9, owner]
        start = jnp.where(kind == 0, 0, jnp.where(kind == 1, to_next, passed))
        stop = jnp.where(kind == 0, to_next, jnp.where(kind == 1, passed, first + count))
        seat = jnp.where(kind == 0, after, jnp.where(kind == 1, before, owner))
        low = jnp.where(
            kind == 0,
            -table[10, after],
            jnp.where(
                kind == 1,
                to_next - table[10, before] - table[8, lax.rem(before + (n_seq - 1), n_seq)],
                passed,
            ),
        )
        away = lax.rem(here - seat + n_seq, n_seq)
        for k in range(n_seq):

            @pl.when(away == k)
            def _(k=k):
                def put(source, lowest):
                    def copy(i):
                        path[level, grain(i), :] = source[grain(first + i - lowest), :]

                    return copy

                edge = low + half
                moved(
                    count, start - first, jnp.minimum(stop, edge) - first, put(sources[2 * k], low)
                )
                moved(
                    count,
                    jnp.maximum(start, edge) - first,
                    stop - first,
                    put(sources[2 * k + 1], edge),
                )

        return carry

    lax.fori_loop(0, 9, piece, 0)


def attention_kernel(
    n_tensor, order, table, groups, branch_of, buckets, weights, query, key, value, path, out, end, own, bias
):
    seq_index = lax.axis_index("seq")
    tensor_index = lax.axis_index("tensor")
    rows, width = out.shape
    heads = width // HEAD
    cap = path.shape[1]
    block = rows // n_tensor
    for number, which in enumerate(order):
        seat = lax.bitwise_xor(tensor_index, jnp.int32(which))
        target = pl.ds(pl.multiple_of(seat * block, block), block)
        for place, source in enumerate((query, key, value)):
            own[target, place * width : (place + 1) * width] = source[
                number * block : (number + 1) * block, :
            ]
    group = groups[0, seq_index]
    counts = [table[0, n] for n in (0, 1 + branch_of[0, group], 1 + BRANCHES + group)]
    starts = [jnp.int32(0), counts[0], counts[0] + counts[1]]
    base = counts[0] + counts[1] + counts[2]
    rels = buckets.shape[1]
    bucket = jnp.broadcast_to(buckets[...], (heads, rels))
    reversed_bias = jnp.zeros((heads, rels), jnp.float32)
    for b in range(weights.shape[1]):
        reversed_bias = jnp.where(bucket == b, weights[:, b : b + 1], reversed_bias)
    half = rels // 2
    window = 2 * rows
    for part in range(4):
        shift = (starts[part] - base) if part < 3 else jnp.int32(0)
        turn = half + 1 + shift
        turned = pltpu.roll(reversed_bias, lax.rem(turn + rels, rels), 1)
        bias[part] = jnp.concatenate([turned[:, :rows], turned[:, rels - rows :]], axis=1)
    key_row = iota((cap, 2 * rows), 0)
    half_row = iota((2 * HEAD, rows), 0) < HEAD

    def one_pair(pair, carry):
        def columns(offset):
            return pl.ds(pl.multiple_of(offset + pair * 2 * HEAD, 2 * HEAD), 2 * HEAD)

        query_t = jnp.transpose(own[:, columns(0)].astype(jnp.float32))
        query_t = jnp.concatenate(
            [jnp.where(half_row, query_t, 0.0), jnp.where(half_row, 0.0, query_t)], axis=1
        ).astype(jnp.bfloat16)
        scores = []
        for part in range(4):
            keys = path[part, :, columns(0)] if part < 3 else own[:, columns(width)]
            score = jnp.dot(keys, query_t, preferred_element_type=jnp.float32)
            slabs = []
            for head in range(2):
                line = jnp.broadcast_to(
                    bias[part, pl.ds(2 * pair + head, 1), :], (rows // 2, window)
                )
                rolled = pltpu.roll(line, 0, 1, stride=1, stride_axis=0)
                lower = jnp.concatenate(
                    [rolled[:, window - rows // 2 :], rolled[:, : rows // 2]], axis=1
                )
                slabs.append(jnp.concatenate([rolled[:, :rows], lower], axis=0))
            score = score + jnp.concatenate(slabs, axis=1)
            if part < 3:
                score = jnp.where(key_row < counts[part], score, -1e30)
            scores.append(score)
        peak = jnp.max(scores[0], axis=0, keepdims=True)
        for score in scores[1:]:
            peak = jnp.maximum(peak, jnp.max(score, axis=0, keepdims=True))
        total = jnp.zeros_like(peak)
        summed = jnp.zeros((2 * HEAD, 2 * rows), jnp.float32)
        for part in range(4):
            chance = jnp.exp(scores[part] - peak)
            total = total + jnp.sum(chance, axis=0, keepdims=True)
            values = path[part, :, columns(width)] if part < 3 else own[:, columns(2 * width)]
            summed = summed + lax.dot_general(
                values,
                chance.astype(jnp.bfloat16),
                (((0,), (0,)), ((), ())),
                preferred_element_type=jnp.float32,
            )
        scaled = summed / total
        both = jnp.concatenate([scaled[:HEAD, :rows], scaled[HEAD:, rows:]], axis=0)
        own[:, columns(0)] = jnp.transpose(both).astype(jnp.bfloat16)
        return carry

    lax.fori_loop(0, heads // 2, one_pair, 0)
    for number, which in enumerate(order):
        seat = lax.bitwise_xor(tensor_index, jnp.int32(which))
        out[number * block : (number + 1) * block, :] = own[
            pl.ds(pl.multiple_of(seat * block, block), block), :width
        ]
    end[...] = own[rows - GRAIN :, :width]


def vmem(count=1):
    return [pl.BlockSpec(memory_space=pltpu.VMEM)] * count


def smem(count=1):
    return [pl.BlockSpec(memory_space=pltpu.SMEM)] * count


def gather_blocks(own, size, order):
    blocks = {0: own}
    for i in sorted(range(1, size), key=lambda i: (bin(i).count("1"), -i)):
        low = i & -i
        blocks[i] = lax.ppermute(blocks[i ^ low], "tensor", xor_pairs(size, low))
    return [blocks[i] for i in order]


def pair_fold(value, size, join):
    return join([value, lax.ppermute(value, "seq", xor_pairs(size, 1))])


def seq_fold(value, size, join):
    return pairs_fold(pair_fold(value, size, join), size, join)


def pairs_fold(value, size, join):
    return join(
        [value] + [lax.ppermute(value, "seq", xor_pairs(size, i)) for i in range(2, size, 2)]
    )


def tensor_sum(value, size, kind):
    mask = 1
    while mask < size:
        sent = value.astype(kind)
        arrived = lax.ppermute(sent, "tensor", xor_pairs(size, mask))
        value = sent.astype(jnp.float32) + arrived.astype(jnp.float32)
        mask *= 2
    return value


def scatter_sum(sent, held, added, size, other=None):
    block = 2 * held.shape[0] // size
    arrived = lax.ppermute(sent, "tensor", xor_pairs(size, 1))
    sums = added + held[-block:] + arrived[-block:].astype(jnp.float32)
    total = held[:-block] + arrived[:-block].astype(jnp.float32)
    mask = 2
    while mask < size:
        count = total.shape[0] // block + 1
        first = total[: count // 2 * block].astype(jnp.bfloat16)
        if other is not None and mask == 2:
            first, other = lax.optimization_barrier((first, other))
        arrived = lax.ppermute(first, "tensor", xor_pairs(size, mask))
        sums = sums + arrived[-block:].astype(jnp.float32)
        total = total[count // 2 * block :] + arrived[:-block].astype(jnp.float32)
        mask *= 2
    return sums if other is None else (sums, other)


def logits_kernel(rows, words, out):
    out[...] = lax.dot_general(
        rows[...], words[...], (((1,), (1,)), ((), ())), preferred_element_type=jnp.float32
    )


def ring_branch(
    rows, n_seq, n_tensor, cap, table, kept, from_before, from_after, groups, branch_of, hidden, gain, weights
):
    width = kept.shape[1]
    limit = pltpu.CompilerParams(vmem_limit_bytes=32 * MIB)
    left, right = pl.pallas_call(
        functools.partial(merge_kernel, n_seq),
        grid=(1,),
        out_shape=[jax.ShapeDtypeStruct((rows // 2, width), kept.dtype)] * 2,
        in_specs=smem() + [pl.BlockSpec((rows, width), lambda i: (0, 0))] + vmem(2),
        out_specs=vmem(2),
        compiler_params=limit,
    )(table, kept, from_before, from_after)
    left, right, hidden = lax.optimization_barrier((left, right, hidden))
    sources = [None] * (2 * n_seq)
    sources[0], sources[1] = left, right
    moving = [[left, right], [left, right]]
    for hop in range(1, n_seq // 2 + 1):
        for way in range(2):
            pairs = ring_pairs(n_seq, 1 if way == 0 else -1)
            for half in range(2):
                if hop == n_seq // 2 and way != half:
                    continue
                moving[way][half] = lax.ppermute(moving[way][half], "seq", pairs)
                away = hop if way == 0 else n_seq - hop
                sources[2 * away + half] = moving[way][half]
    normed = rms_scale(hidden, gain).astype(jnp.bfloat16)
    normed = jnp.concatenate(gather_blocks(normed, n_tensor, block_order(n_tensor)), axis=0)
    projected = [
        jnp.dot(normed, weight, preferred_element_type=jnp.float32).astype(jnp.bfloat16)
        for weight in weights
    ]
    path = pl.pallas_call(
        functools.partial(assemble_kernel, n_seq),
        out_shape=jax.ShapeDtypeStruct((3, cap, width), kept.dtype),
        in_specs=smem(3) + vmem(len(sources)),
        out_specs=vmem()[0],
        compiler_params=limit,
    )(table, groups, branch_of, *sources)
    return (path, *projected)


def per_device(
    hidden,
    attn_gain,
    attn_query,
    attn_key,
    attn_value,
    attn_out,
    ff_gain,
    ff_gate,
    ff_up,
    ff_down,
    final_gain,
    embedding,
    rel_weight,
    bucket_table,
    prefix_kv,
    node_lengths,
    group_branch,
    node_slot,
    request_group,
):
    n_seq = lax.axis_size("seq")
    n_tensor = lax.axis_size("tensor")
    tensor_index = lax.axis_index("tensor")
    own_rows, width = hidden.shape
    assert request_group.shape[0] == n_seq
    order = block_order(n_tensor)
    slots_here, cap, head_cols = prefix_kv.shape[1:]
    most = slots_here * cap
    classes = [most] + [c for c in CLASSES if c < most]
    passed = min(PASSED, most)
    groups = request_group[None, :]
    branch_of = group_branch[None, :]
    table = pl.pallas_call(
        functools.partial(plan_kernel, n_seq, slots_here, passed, classes),
        out_shape=jax.ShapeDtypeStruct((16, 128), jnp.int32),
        in_specs=vmem(4),
        out_specs=vmem()[0],
    )(node_lengths[None, :], node_slot[None, :], branch_of, groups)
    onward, backward, kept = pl.pallas_call(
        functools.partial(pack_kernel, n_seq, node_lengths.shape[0]),
        out_shape=[
            jax.ShapeDtypeStruct((size, 2 * head_cols), prefix_kv.dtype)
            for size in (passed, passed, most)
        ],
        in_specs=smem() + vmem(),
        out_specs=vmem(3),
        compiler_params=pltpu.CompilerParams(vmem_limit_bytes=32 * MIB),
    )(table, prefix_kv)
    from_before = lax.ppermute(onward, "seq", ring_pairs(n_seq, 1))
    from_after = lax.ppermute(backward, "seq", ring_pairs(n_seq, -1))
    path, *projected = lax.switch(
        table[11, 0],
        [functools.partial(ring_branch, c, n_seq, n_tensor, cap) for c in classes],
        table,
        kept,
        from_before,
        from_after,
        groups,
        branch_of,
        hidden,
        attn_gain,
        (attn_query, attn_key, attn_value),
    )
    n_rows = own_rows * n_tensor
    attn, attn_end = pl.pallas_call(
        functools.partial(attention_kernel, n_tensor, order),
        out_shape=[
            jax.ShapeDtypeStruct((size, head_cols), jnp.bfloat16) for size in (n_rows, GRAIN)
        ],
        in_specs=smem(3) + vmem(6),
        out_specs=vmem(2),
        scratch_shapes=[
            pltpu.VMEM((n_rows, 3 * head_cols), jnp.bfloat16),
            pltpu.VMEM((4, head_cols // HEAD, 2 * n_rows), jnp.float32),
        ],
        compiler_params=pltpu.CompilerParams(vmem_limit_bytes=32 * MIB),
    )(
        table,
        groups,
        branch_of,
        bucket_table[::-1][None, :],
        jnp.transpose(rel_weight),
        *projected,
        path,
    )
    half = n_rows // 2
    sent = jnp.dot(attn[:half], attn_out, preferred_element_type=jnp.float32).astype(jnp.bfloat16)
    held = jnp.dot(attn[half:], attn_out, preferred_element_type=jnp.float32)
    keeper = tensor_index == n_tensor - 1
    ends = jnp.concatenate([attn_end[GRAIN - 1 :], hidden[own_rows - 1 :]], axis=1)
    ends, sent = lax.optimization_barrier((ends, sent))
    rows_join = functools.partial(jnp.concatenate, axis=0)
    ends = pair_fold(ends, n_seq, rows_join)
    mid, ends = scatter_sum(sent, held, hidden.astype(jnp.float32), n_tensor, ends)
    mid = mid.astype(jnp.bfloat16)
    ends = pairs_fold(ends, n_seq, rows_join)
    mid_normed = rms_scale(mid, ff_gain).astype(jnp.bfloat16)
    ends = ends[lax.bitwise_xor(lax.axis_index("seq"), jnp.arange(n_seq))]
    part = jnp.dot(ends[:, :head_cols], attn_out, preferred_element_type=jnp.float32)
    part = part + jnp.where(keeper, ends[:, head_cols:].astype(jnp.float32), 0.0)
    end_mid = tensor_sum(part, n_tensor, jnp.float32).astype(jnp.bfloat16)
    end_normed = rms_scale(end_mid, ff_gain).astype(jnp.bfloat16)
    end_normed = jnp.pad(end_normed, ((0, -n_seq % GRAIN), (0, 0)))
    blocks = gather_blocks(mid_normed, n_tensor, order)
    blocks = blocks[: n_tensor // 2] + [end_normed] + blocks[n_tensor // 2 :]
    inner = gated(jnp.concatenate(blocks, axis=0), ff_gate, ff_up)
    sent = jnp.dot(inner[:-half], ff_down, preferred_element_type=jnp.float32)
    held = jnp.dot(inner[-half:], ff_down, preferred_element_type=jnp.float32)
    sent, held = lax.optimization_barrier((sent, held))
    part, sent = sent[half : half + n_seq], sent[:half].astype(jnp.bfloat16)
    end_out = end_mid.astype(jnp.float32) + tensor_sum(part, n_tensor, jnp.bfloat16)
    hidden_out = scatter_sum(sent, held, mid.astype(jnp.float32), n_tensor).astype(jnp.bfloat16)
    last_rows = end_out.astype(jnp.bfloat16).astype(jnp.float32)
    mean_square = jnp.mean(last_rows * last_rows, axis=1)
    last_rms = jnp.sqrt(mean_square)
    final_rows = (last_rows * lax.rsqrt(mean_square + 1e-06)[:, None] * final_gain).astype(
        jnp.bfloat16
    )
    embed_cols = embedding.shape[1]
    columns = lax.dynamic_slice_in_dim(final_rows, tensor_index * embed_cols, embed_cols, 1)
    logits = lax.dot_general(
        columns, embedding, (((1,), (1,)), ((), ())), preferred_element_type=jnp.float32
    )
    top = jnp.max(tensor_sum(logits, n_tensor, jnp.bfloat16), axis=1)
    top_logit = seq_fold(top, n_seq, functools.partial(functools.reduce, jnp.maximum))
    return (hidden_out, last_rms, top_logit)


def solution(mesh):
    return jax.shard_map(
        per_device,
        mesh=mesh,
        in_specs=(
            P(("seq", "tensor"), None),
            P(),
            P(None, "tensor"),
            P(None, "tensor"),
            P(None, "tensor"),
            P("tensor", None),
            P(),
            P(None, "tensor"),
            P(None, "tensor"),
            P("tensor", None),
            P(),
            P("seq", "tensor"),
            P(None, "tensor"),
            P(),
            P(None, "seq", None, "tensor"),
            P(),
            P(),
            P(),
            P(),
        ),
        out_specs=(P(("seq", "tensor"), None), P(), P()),
        check_vma=False,
    )
```

```python
import functools

import jax
import jax.numpy as jnp
from jax import lax
from jax.experimental import pallas as pl
from jax.experimental.pallas import tpu as pltpu
from jax.sharding import PartitionSpec as P

BRANCHES = 7
HEAD = 64
GRAIN = 16
MIB = 1 << 20
PASSED = 160
CLASSES = (464, 320, 240, 192, 160, 128)


def rms_scale(values, gain):
    widened = values.astype(jnp.float32)
    mean_square = jnp.mean(widened * widened, axis=-1, keepdims=True)
    return widened * lax.rsqrt(mean_square + 1e-06) * gain


def gated(rows, gate, up):
    gate_part = jnp.dot(rows, gate, preferred_element_type=jnp.float32)
    up_part = jnp.dot(rows, up, preferred_element_type=jnp.float32)
    return (jax.nn.gelu(gate_part, approximate=True) * up_part).astype(jnp.bfloat16)


def xor_pairs(size, mask):
    return [(i, i ^ mask) for i in range(size)]


def ring_place(index, size):
    half = lax.shift_right_logical(index, jnp.int32(1))
    return jnp.where(lax.bitwise_and(index, jnp.int32(1)) == 0, half, size - 1 - half)


def ring_pairs(size, step):
    order = list(range(0, size, 2)) + list(range(1, size, 2))[::-1]
    return [(order[i], order[(i + step) % size]) for i in range(size)]


def block_order(size):
    bits = size.bit_length() - 1
    return sorted(range(size), key=lambda i: -int(format(i, "b").zfill(bits)[::-1], 2))


def iota(shape, axis):
    return lax.broadcasted_iota(jnp.int32, shape, axis)


def plan_kernel(n_seq, slots_here, passed, classes, lengths, slots, branch_of, groups, table):
    nodes = lengths.shape[1]
    requests = groups.shape[1]
    eye = iota((nodes, nodes), 0) == iota((nodes, nodes), 1)
    seq_eye = iota((n_seq, n_seq), 0) == iota((n_seq, n_seq), 1)

    def column(row):
        return jnp.sum(jnp.where(eye, row, 0), axis=1, keepdims=True)

    def seq_row(col):
        return jnp.sum(jnp.where(seq_eye, col, 0), axis=0, keepdims=True)

    slot = slots[...]
    owner = jnp.zeros_like(slot)
    for k in range(1, n_seq):
        owner = owner + (slot >= k * slots_here).astype(jnp.int32)
    place = ring_place(owner, n_seq)
    req_eye = iota((requests, requests), 0) == iota((requests, requests), 1)
    group = jnp.sum(jnp.where(req_eye, groups[...], 0), axis=1, keepdims=True)
    n_groups = branch_of.shape[1]
    branch = jnp.sum(
        jnp.where(iota((requests, n_groups), 1) == group, branch_of[...], 0), axis=1, keepdims=True
    )
    node = iota((requests, nodes), 1)
    need = (node == 0) | (node == 1 + branch) | (node == 1 + BRANCHES + group)
    seats = ring_place(iota((requests, nodes), 0), n_seq)
    needed = jnp.max((need & (seats != place)).astype(jnp.int32), axis=0, keepdims=True)
    grains = needed * lax.shift_right_logical(lengths[...] + (GRAIN - 1), jnp.int32(4))
    earlier = iota((nodes, nodes), 0) < iota((nodes, nodes), 1)
    before = (column(place) == place) & earlier
    first = jnp.sum(jnp.where(before, column(grains), 0), axis=0, keepdims=True)
    held = jnp.sum(
        jnp.where(iota((n_seq, nodes), 0) == place, grains, 0), axis=1, keepdims=True
    )
    every = jnp.sum(held, axis=0, keepdims=True)
    upto = iota((n_seq, n_seq), 1) <= iota((n_seq, n_seq), 0)
    surplus = n_seq * seq_row(held) - every
    running = jnp.sum(jnp.where(upto, surplus, 0), axis=1, keepdims=True)
    middle = lax.shift_right_arithmetic(
        jnp.max(running, axis=0, keepdims=True) + jnp.min(running, axis=0, keepdims=True),
        jnp.int32(1),
    )
    flow = lax.shift_right_arithmetic(
        running - middle + n_seq // 2, jnp.int32(n_seq.bit_length() - 1)
    )
    most = passed // GRAIN
    flow = jnp.minimum(jnp.maximum(flow, -most), most)
    before_me = iota((n_seq, n_seq), 1) == lax.rem(
        iota((n_seq, n_seq), 0) + (n_seq - 1), jnp.int32(n_seq)
    )
    after_me = iota((n_seq, n_seq), 1) == lax.rem(
        iota((n_seq, n_seq), 0) + 1, jnp.int32(n_seq)
    )

    def from_seat(which, col):
        return jnp.sum(jnp.where(which, seq_row(col), 0), axis=1, keepdims=True)

    onward = jnp.minimum(jnp.maximum(flow, 0), held)
    backward = jnp.minimum(jnp.maximum(-from_seat(before_me, flow), 0), held - onward)
    kept = held - onward - backward
    block = kept + from_seat(before_me, onward) + from_seat(after_me, backward)
    largest = jnp.max(block, axis=0, keepdims=True) * GRAIN
    choice = jnp.zeros((1, 1), jnp.int32)
    for number, rows in enumerate(classes):
        choice = jnp.where(largest <= rows, number, choice)
    table[...] = jnp.zeros_like(table)
    for number, row in enumerate((lengths[...], place, first, slot - owner * slots_here, grains)):
        table[number : number + 1, :nodes] = row
    for number, col in enumerate((onward, backward, kept)):
        table[8 + number : 9 + number, :n_seq] = seq_row(col)
    table[11:12, :] = jnp.broadcast_to(choice, (1, table.shape[1]))


def moved(count, start, stop, copy):
    def step(i, carry):
        copy(i)
        return carry

    lax.fori_loop(jnp.maximum(start, 0), jnp.minimum(stop, count), step, 0)


def grain(i):
    return pl.ds(pl.multiple_of(i * GRAIN, GRAIN), GRAIN)


def pack_kernel(n_seq, nodes, table, cache, onward, backward, kept):
    here = ring_place(lax.axis_index("seq"), n_seq)
    width = cache.shape[3]
    to_next = table[8, here]
    passed = to_next + table[9, here]

    def one_node(n, carry):
        @pl.when((table[1, n] == here) & (table[4, n] > 0))
        def _():
            slot = table[3, n]
            count = table[4, n]
            first = table[2, n]

            def put(target, low):
                def copy(i):
                    target[grain(first + i - low), :width] = cache[0, slot, grain(i), :]
                    target[grain(first + i - low), width:] = cache[1, slot, grain(i), :]

                return copy

            moved(count, 0, to_next - first, put(onward, 0))
            moved(count, to_next - first, passed - first, put(backward, to_next))
            moved(count, passed - first, count, put(kept, passed))

        return carry

    lax.fori_loop(0, nodes, one_node, 0)


def merge_kernel(n_seq, table, kept, from_before, from_after, left, right):
    here = ring_place(lax.axis_index("seq"), n_seq)
    before = lax.rem(here + (n_seq - 1), n_seq)
    after = lax.rem(here + 1, n_seq)
    half = left.shape[0] // GRAIN
    left[...] = kept[: left.shape[0], :]
    right[...] = kept[left.shape[0] :, :]
    at = table[10, here]
    for source, count in ((from_before, table[8, before]), (from_after, table[9, after])):

        def to_left(i, source=source, at=at):
            left[grain(at + i), :] = source[grain(i), :]

        def to_right(i, source=source, at=at):
            right[grain(at + i - half), :] = source[grain(i), :]

        moved(count, 0, half - at, to_left)
        moved(count, half - at, count, to_right)
        at = at + count


def assemble_kernel(n_seq, table, groups, branch_of, *refs):
    sources, (cache, path, sem) = refs[:-3], refs[-3:]
    half = sources[0].shape[0] // GRAIN
    seq_index = lax.axis_index("seq")
    here = ring_place(seq_index, n_seq)
    path[...] = jnp.zeros_like(path)
    group = groups[0, seq_index]
    width = cache.shape[3]
    for level, n in enumerate(
        (jnp.int32(0), 1 + branch_of[0, group], 1 + BRANCHES + group)
    ):

        @pl.when(table[1, n] == here)
        def _(level=level, n=n):
            for part in range(2):
                copy = pltpu.make_async_copy(
                    cache.at[part, table[3, n]],
                    path.at[level, :, part * width : (part + 1) * width],
                    sem.at[part],
                )
                copy.start()
                copy.wait()

    def piece(number, carry):
        level = lax.div(number, 3)
        kind = lax.rem(number, 3)
        n = jnp.where(
            level == 0, 0, jnp.where(level == 1, 1 + branch_of[0, group], 1 + BRANCHES + group)
        )
        owner = table[1, n]
        count = jnp.where(owner == here, 0, table[4, n])
        first = table[2, n]
        before = lax.rem(owner + (n_seq - 1), n_seq)
        after = lax.rem(owner + 1, n_seq)
        to_next = table[8, owner]
        passed = to_next + table[9, owner]
        start = jnp.where(kind == 0, 0, jnp.where(kind == 1, to_next, passed))
        stop = jnp.where(kind == 0, to_next, jnp.where(kind == 1, passed, first + count))
        seat = jnp.where(kind == 0, after, jnp.where(kind == 1, before, owner))
        low = jnp.where(
            kind == 0,
            -table[10, after],
            jnp.where(
                kind == 1,
                to_next - table[10, before] - table[8, lax.rem(before + (n_seq - 1), n_seq)],
                passed,
            ),
        )
        away = lax.rem(here - seat + n_seq, n_seq)
        for k in range(n_seq):

            @pl.when(away == k)
            def _(k=k):
                def put(source, lowest):
                    def copy(i):
                        path[level, grain(i), :] = source[grain(first + i - lowest), :]

                    return copy

                edge = low + half
                moved(
                    count, start - first, jnp.minimum(stop, edge) - first, put(sources[2 * k], low)
                )
                moved(
                    count,
                    jnp.maximum(start, edge) - first,
                    stop - first,
                    put(sources[2 * k + 1], edge),
                )

        return carry

    lax.fori_loop(0, 9, piece, 0)


def attention_kernel(
    n_tensor, order, table, groups, branch_of, buckets, weights, query, key, value, path, out, end, own, bias
):
    seq_index = lax.axis_index("seq")
    tensor_index = lax.axis_index("tensor")
    rows, width = out.shape
    heads = width // HEAD
    cap = path.shape[1]
    block = rows // n_tensor
    for number, which in enumerate(order):
        seat = lax.bitwise_xor(tensor_index, jnp.int32(which))
        target = pl.ds(pl.multiple_of(seat * block, block), block)
        for place, source in enumerate((query, key, value)):
            own[target, place * width : (place + 1) * width] = source[
                number * block : (number + 1) * block, :
            ]
    group = groups[0, seq_index]
    counts = [table[0, n] for n in (0, 1 + branch_of[0, group], 1 + BRANCHES + group)]
    starts = [jnp.int32(0), counts[0], counts[0] + counts[1]]
    base = counts[0] + counts[1] + counts[2]
    rels = buckets.shape[1]
    bucket = jnp.broadcast_to(buckets[...], (heads, rels))
    reversed_bias = jnp.zeros((heads, rels), jnp.float32)
    for b in range(weights.shape[1]):
        reversed_bias = jnp.where(bucket == b, weights[:, b : b + 1], reversed_bias)
    half = rels // 2
    window = 2 * rows
    for part in range(4):
        shift = (starts[part] - base) if part < 3 else jnp.int32(0)
        turn = half + 1 + shift
        turned = pltpu.roll(reversed_bias, lax.rem(turn + rels, rels), 1)
        bias[part] = jnp.concatenate([turned[:, :rows], turned[:, rels - rows :]], axis=1)
    key_row = iota((cap, 2 * rows), 0)
    half_row = iota((2 * HEAD, rows), 0) < HEAD

    def one_pair(pair, carry):
        def columns(offset):
            return pl.ds(pl.multiple_of(offset + pair * 2 * HEAD, 2 * HEAD), 2 * HEAD)

        query_t = jnp.transpose(own[:, columns(0)].astype(jnp.float32))
        query_t = jnp.concatenate(
            [jnp.where(half_row, query_t, 0.0), jnp.where(half_row, 0.0, query_t)], axis=1
        ).astype(jnp.bfloat16)
        scores = []
        for part in range(4):
            keys = path[part, :, columns(0)] if part < 3 else own[:, columns(width)]
            score = jnp.dot(keys, query_t, preferred_element_type=jnp.float32)
            slabs = []
            for head in range(2):
                line = jnp.broadcast_to(
                    bias[part, pl.ds(2 * pair + head, 1), :], (rows // 2, window)
                )
                rolled = pltpu.roll(line, 0, 1, stride=1, stride_axis=0)
                lower = jnp.concatenate(
                    [rolled[:, window - rows // 2 :], rolled[:, : rows // 2]], axis=1
                )
                slabs.append(jnp.concatenate([rolled[:, :rows], lower], axis=0))
            score = score + jnp.concatenate(slabs, axis=1)
            if part < 3:
                score = jnp.where(key_row < counts[part], score, -1e30)
            scores.append(score)
        peak = jnp.max(scores[0], axis=0, keepdims=True)
        for score in scores[1:]:
            peak = jnp.maximum(peak, jnp.max(score, axis=0, keepdims=True))
        total = jnp.zeros_like(peak)
        summed = jnp.zeros((2 * HEAD, 2 * rows), jnp.float32)
        for part in range(4):
            chance = jnp.exp(scores[part] - peak)
            total = total + jnp.sum(chance, axis=0, keepdims=True)
            values = path[part, :, columns(width)] if part < 3 else own[:, columns(2 * width)]
            summed = summed + lax.dot_general(
                values,
                chance.astype(jnp.bfloat16),
                (((0,), (0,)), ((), ())),
                preferred_element_type=jnp.float32,
            )
        scaled = summed / total
        both = jnp.concatenate([scaled[:HEAD, :rows], scaled[HEAD:, rows:]], axis=0)
        own[:, columns(0)] = jnp.transpose(both).astype(jnp.bfloat16)
        return carry

    lax.fori_loop(0, heads // 2, one_pair, 0)
    for number, which in enumerate(order):
        seat = lax.bitwise_xor(tensor_index, jnp.int32(which))
        out[number * block : (number + 1) * block, :] = own[
            pl.ds(pl.multiple_of(seat * block, block), block), :width
        ]
    end[...] = own[rows - GRAIN :, :width]


def vmem(count=1):
    return [pl.BlockSpec(memory_space=pltpu.VMEM)] * count


def smem(count=1):
    return [pl.BlockSpec(memory_space=pltpu.SMEM)] * count


def gather_blocks(own, size, order):
    blocks = {0: own}
    for i in sorted(range(1, size), key=lambda i: (bin(i).count("1"), -i)):
        low = i & -i
        blocks[i] = lax.ppermute(blocks[i ^ low], "tensor", xor_pairs(size, low))
    return [blocks[i] for i in order]


def pair_fold(value, size, join):
    return join([value, lax.ppermute(value, "seq", xor_pairs(size, 1))])


def seq_fold(value, size, join):
    return pairs_fold(pair_fold(value, size, join), size, join)


def pairs_fold(value, size, join):
    return join(
        [value] + [lax.ppermute(value, "seq", xor_pairs(size, i)) for i in range(2, size, 2)]
    )


def tensor_sum(value, size, kind):
    mask = 1
    while mask < size:
        sent = value.astype(kind)
        arrived = lax.ppermute(sent, "tensor", xor_pairs(size, mask))
        value = sent.astype(jnp.float32) + arrived.astype(jnp.float32)
        mask *= 2
    return value


def scatter_sum(sent, held, added, size, other=None):
    block = 2 * held.shape[0] // size
    arrived = lax.ppermute(sent, "tensor", xor_pairs(size, 1))
    sums = added + held[-block:] + arrived[-block:].astype(jnp.float32)
    total = held[:-block] + arrived[:-block].astype(jnp.float32)
    mask = 2
    while mask < size:
        count = total.shape[0] // block + 1
        first = total[: count // 2 * block].astype(jnp.bfloat16)
        if other is not None and mask == 2:
            first, other = lax.optimization_barrier((first, other))
        arrived = lax.ppermute(first, "tensor", xor_pairs(size, mask))
        sums = sums + arrived[-block:].astype(jnp.float32)
        total = total[count // 2 * block :] + arrived[:-block].astype(jnp.float32)
        mask *= 2
    return sums if other is None else (sums, other)


def logits_kernel(rows, words, out):
    out[...] = lax.dot_general(
        rows[...], words[...], (((1,), (1,)), ((), ())), preferred_element_type=jnp.float32
    )


def ring_branch(
    rows, n_seq, n_tensor, table, kept, from_before, from_after, groups, branch_of, prefix_kv, hidden, gain, weights
):
    width, cap = kept.shape[1], prefix_kv.shape[2]
    limit = pltpu.CompilerParams(vmem_limit_bytes=32 * MIB)
    lower = (rows // GRAIN + 1) // 2 * GRAIN
    sizes = (lower, rows - lower)
    left, right = pl.pallas_call(
        functools.partial(merge_kernel, n_seq),
        grid=(1,),
        out_shape=[jax.ShapeDtypeStruct((size, width), kept.dtype) for size in sizes],
        in_specs=smem() + [pl.BlockSpec((rows, width), lambda i: (0, 0))] + vmem(2),
        out_specs=vmem(2),
        compiler_params=limit,
    )(table, kept, from_before, from_after)
    left, right, hidden = lax.optimization_barrier((left, right, hidden))
    sources = [None] * (2 * n_seq)
    sources[0], sources[1] = left, right
    moving = [[left, right], [left, right]]
    for hop in range(1, n_seq // 2 + 1):
        for way in range(2):
            pairs = ring_pairs(n_seq, 1 if way == 0 else -1)
            for half in range(2):
                if hop == n_seq // 2 and way != half:
                    continue
                moving[way][half] = lax.ppermute(moving[way][half], "seq", pairs)
                away = hop if way == 0 else n_seq - hop
                sources[2 * away + half] = moving[way][half]
    normed = rms_scale(hidden, gain).astype(jnp.bfloat16)
    normed = jnp.concatenate(gather_blocks(normed, n_tensor, block_order(n_tensor)), axis=0)
    projected = [
        jnp.dot(normed, weight, preferred_element_type=jnp.float32).astype(jnp.bfloat16)
        for weight in weights
    ]
    path = pl.pallas_call(
        functools.partial(assemble_kernel, n_seq),
        out_shape=jax.ShapeDtypeStruct((3, cap, width), kept.dtype),
        in_specs=smem(3) + vmem(len(sources)) + [pl.BlockSpec(memory_space=pl.ANY)],
        out_specs=vmem()[0],
        scratch_shapes=[pltpu.SemaphoreType.DMA((2,))],
        compiler_params=limit,
    )(table, groups, branch_of, *sources, prefix_kv)
    return (path, *projected)


def per_device(
    hidden,
    attn_gain,
    attn_query,
    attn_key,
    attn_value,
    attn_out,
    ff_gain,
    ff_gate,
    ff_up,
    ff_down,
    final_gain,
    embedding,
    rel_weight,
    bucket_table,
    prefix_kv,
    node_lengths,
    group_branch,
    node_slot,
    request_group,
):
    n_seq = lax.axis_size("seq")
    n_tensor = lax.axis_size("tensor")
    tensor_index = lax.axis_index("tensor")
    own_rows, width = hidden.shape
    assert request_group.shape[0] == n_seq
    order = block_order(n_tensor)
    slots_here, cap, head_cols = prefix_kv.shape[1:]
    most = slots_here * cap
    classes = [most] + [c for c in CLASSES if c < most]
    passed = min(PASSED, most)
    groups = request_group[None, :]
    branch_of = group_branch[None, :]
    table = pl.pallas_call(
        functools.partial(plan_kernel, n_seq, slots_here, passed, classes),
        out_shape=jax.ShapeDtypeStruct((16, 128), jnp.int32),
        in_specs=vmem(4),
        out_specs=vmem()[0],
    )(node_lengths[None, :], node_slot[None, :], branch_of, groups)
    onward, backward, kept = pl.pallas_call(
        functools.partial(pack_kernel, n_seq, node_lengths.shape[0]),
        out_shape=[
            jax.ShapeDtypeStruct((size, 2 * head_cols), prefix_kv.dtype)
            for size in (passed, passed, most)
        ],
        in_specs=smem() + vmem(),
        out_specs=vmem(3),
        compiler_params=pltpu.CompilerParams(vmem_limit_bytes=32 * MIB),
    )(table, prefix_kv)
    from_before = lax.ppermute(onward, "seq", ring_pairs(n_seq, 1))
    from_after = lax.ppermute(backward, "seq", ring_pairs(n_seq, -1))
    path, *projected = lax.switch(
        table[11, 0],
        [functools.partial(ring_branch, c, n_seq, n_tensor) for c in classes],
        table,
        kept,
        from_before,
        from_after,
        groups,
        branch_of,
        prefix_kv,
        hidden,
        attn_gain,
        (attn_query, attn_key, attn_value),
    )
    n_rows = own_rows * n_tensor
    attn, attn_end = pl.pallas_call(
        functools.partial(attention_kernel, n_tensor, order),
        out_shape=[
            jax.ShapeDtypeStruct((size, head_cols), jnp.bfloat16) for size in (n_rows, GRAIN)
        ],
        in_specs=smem(3) + vmem(6),
        out_specs=vmem(2),
        scratch_shapes=[
            pltpu.VMEM((n_rows, 3 * head_cols), jnp.bfloat16),
            pltpu.VMEM((4, head_cols // HEAD, 2 * n_rows), jnp.float32),
        ],
        compiler_params=pltpu.CompilerParams(vmem_limit_bytes=32 * MIB),
    )(
        table,
        groups,
        branch_of,
        bucket_table[::-1][None, :],
        jnp.transpose(rel_weight),
        *projected,
        path,
    )
    half = n_rows // 2
    sent = jnp.dot(attn[:half], attn_out, preferred_element_type=jnp.float32).astype(jnp.bfloat16)
    held = jnp.dot(attn[half:], attn_out, preferred_element_type=jnp.float32)
    keeper = tensor_index == n_tensor - 1
    ends = jnp.concatenate([attn_end[GRAIN - 1 :], hidden[own_rows - 1 :]], axis=1)
    ends, sent = lax.optimization_barrier((ends, sent))
    rows_join = functools.partial(jnp.concatenate, axis=0)
    ends = pair_fold(ends, n_seq, rows_join)
    mid, ends = scatter_sum(sent, held, hidden.astype(jnp.float32), n_tensor, ends)
    mid = mid.astype(jnp.bfloat16)
    ends = pairs_fold(ends, n_seq, rows_join)
    mid_normed = rms_scale(mid, ff_gain).astype(jnp.bfloat16)
    ends = ends[lax.bitwise_xor(lax.axis_index("seq"), jnp.arange(n_seq))]
    part = jnp.dot(ends[:, :head_cols], attn_out, preferred_element_type=jnp.float32)
    part = part + jnp.where(keeper, ends[:, head_cols:].astype(jnp.float32), 0.0)
    end_mid = tensor_sum(part, n_tensor, jnp.float32).astype(jnp.bfloat16)
    end_normed = rms_scale(end_mid, ff_gain).astype(jnp.bfloat16)
    end_normed = jnp.pad(end_normed, ((0, -n_seq % GRAIN), (0, 0)))
    blocks = gather_blocks(mid_normed, n_tensor, order)
    blocks = blocks[: n_tensor // 2] + [end_normed] + blocks[n_tensor // 2 :]
    inner = gated(jnp.concatenate(blocks, axis=0), ff_gate, ff_up)
    sent = jnp.dot(inner[:-half], ff_down, preferred_element_type=jnp.float32)
    held = jnp.dot(inner[-half:], ff_down, preferred_element_type=jnp.float32)
    sent, held = lax.optimization_barrier((sent, held))
    part, sent = sent[half : half + n_seq], sent[:half].astype(jnp.bfloat16)
    end_out = end_mid.astype(jnp.float32) + tensor_sum(part, n_tensor, jnp.bfloat16)
    hidden_out = scatter_sum(sent, held, mid.astype(jnp.float32), n_tensor).astype(jnp.bfloat16)
    last_rows = end_out.astype(jnp.bfloat16).astype(jnp.float32)
    mean_square = jnp.mean(last_rows * last_rows, axis=1)
    last_rms = jnp.sqrt(mean_square)
    final_rows = (last_rows * lax.rsqrt(mean_square + 1e-06)[:, None] * final_gain).astype(
        jnp.bfloat16
    )
    embed_cols = embedding.shape[1]
    columns = lax.dynamic_slice_in_dim(final_rows, tensor_index * embed_cols, embed_cols, 1)
    logits = lax.dot_general(
        columns, embedding, (((1,), (1,)), ((), ())), preferred_element_type=jnp.float32
    )
    top = jnp.max(tensor_sum(logits, n_tensor, jnp.bfloat16), axis=1)
    top_logit = seq_fold(top, n_seq, functools.partial(functools.reduce, jnp.maximum))
    return (hidden_out, last_rms, top_logit)


def solution(mesh):
    return jax.shard_map(
        per_device,
        mesh=mesh,
        in_specs=(
            P(("seq", "tensor"), None),
            P(),
            P(None, "tensor"),
            P(None, "tensor"),
            P(None, "tensor"),
            P("tensor", None),
            P(),
            P(None, "tensor"),
            P(None, "tensor"),
            P("tensor", None),
            P(),
            P("seq", "tensor"),
            P(None, "tensor"),
            P(),
            P(None, "seq", None, "tensor"),
            P(),
            P(),
            P(),
            P(),
        ),
        out_specs=(P(("seq", "tensor"), None), P(), P()),
        check_vma=False,
    )
```
